32 devices in a mesh: slot: 4 (over y, core), blk: 8 (over z, x).
Axes of the slice: x: 2, y: 2, z: 4, core: 2. Of those that a mesh axis runs over, the one named last changes fastest.
Arguments:
- activations: bfloat16 [16, 1024, 1024], P('slot', 'blk'), may hold values from -6 to 6
- cotangent: bfloat16 [16, 1024, 1024], P('slot', 'blk'), may hold values from -6 to 6
- norm_gains: float32 [2, 1024], replicated, may hold values from 0.5 to 1.5
- norm_shifts: float32 [2, 1024], replicated, may hold values from -0.6 to 0.6
- w_qkv: bfloat16 [1024, 3072], replicated, may hold values from -0.1875 to 0.1875
- query_value_bias: float32 [2, 1024], replicated, may hold values from -3 to 3
- w_out: bfloat16 [1024, 1024], replicated, may hold values from -0.75 to 0.75
- resid_bias: float32 [2, 1024], replicated, may hold values from -1.2 to 1.2
- w_fc: bfloat16 [1024, 4096], replicated, may hold values from -0.1875 to 0.1875
- fc_bias: float32 [4096], replicated, may hold values from -3 to 3
- w_proj: bfloat16 [4096, 1024], replicated, may hold values from -0.09375 to 0.09375
- doc_ids: int32 [16, 1024], P('slot', 'blk'), may hold values from 0 to 1023, as said below
- adapters: float32 [4, 4, 1024], replicated, may hold values from -0.3 to 0.3
- moment_one: float32 [4, 4, 1024], replicated, may hold values from -6 to 6
- moment_two: float32 [4, 4, 1024], replicated, may hold values from 0.0002 to 0.004
Outputs:
- block_output: bfloat16 [16, 1024, 1024], P('slot', 'blk')
- input_grad: bfloat16 [16, 1024, 1024], P('slot', 'blk')
- clipped_grads: float32 [4, 4, 1024], replicated
- new_adapters: float32 [4, 4, 1024], replicated
- new_moment_one: float32 [4, 4, 1024], replicated
- new_moment_two: float32 [4, 4, 1024], replicated
The draws below stay inside these ranges and needn't reach their ends.
Inputs may be any that keep to these rules, and one draw needn't show every extreme that they name: `doc_ids`: A token's number is the position in its slot where its document begins, so numbers never fall along a slot; the last position of every slot is a document of one token. Documents otherwise hold from about 6 to about 40 hundredths of a slot's 1024 tokens (cut ones shorter). In each aligned group of 4 slots, one slot drawn from the seed holds a document that starts within its first 128 positions and ends within its last 128 positions.
All inputs are finite; a program needn't handle non-finite values.
Results may differ from the reference program's by a relative error of at most 0.015.
Values may be sent and summed in bfloat16 or wider, within the bound.
No kernel may reach another device: no remote copies, remote signals or barrier semaphores. Data moves between devices by JAX's collectives and lax.ppermute only.
A program may use at most 256 MiB of HBM per device.

```python
import math
import jax
import jax.numpy as jnp
from jax import lax

MODEL_WIDTH = 1024
HEADS = 16
HEAD_DIM = 64
FF = 4096
RANK = 4
SLOT_LEN = 1024
SLOTS_DEV = 4
SHARD = 128
SLOTS = 16


def draw_doc_ids(key, part):
    key = jax.random.fold_in(key, 11)
    key_start, key_end, key_lengths, key_pick = jax.random.split(key, 4)
    shortest = max(2, SLOT_LEN * 60 // 1024)
    longest = max(shortest + 1, SLOT_LEN * 400 // 1024) + 1
    piece_count = SLOT_LEN // shortest + 2
    lengths = jax.random.randint(key_lengths, (SLOTS, piece_count), shortest, longest).astype(jnp.int32)
    starts = (jnp.cumsum(lengths, axis=1) - lengths).astype(jnp.int32)
    places = jnp.arange(SLOT_LEN, dtype=jnp.int32)[None, :]
    short_bounds = jnp.any(places[:, :, None] == starts[:, None, :], axis=2)
    chosen = jax.random.randint(key_pick, (SLOTS // SLOTS_DEV, 1), 0, SLOTS_DEV)
    within = jnp.arange(SLOTS_DEV, dtype=jnp.int32)[None, :]
    long_slot = (within == chosen).reshape(SLOTS, 1)
    opening = jax.random.randint(key_start, (SLOTS, 1), 0, SHARD)
    closing = jax.random.randint(key_end, (SLOTS, 1), SLOT_LEN - SHARD + 1, SLOT_LEN)
    outside = (places < opening) | (places >= closing)
    long_marks = (places == opening) | (places == closing)
    bounds = jnp.where(long_slot, short_bounds & outside | long_marks, short_bounds)
    bounds = bounds | (places == 0) | (places == SLOT_LEN - 1)
    starts_at = jnp.where(bounds, places, 0).astype(jnp.int32)
    return lax.cummax(starts_at, axis=1).astype(jnp.int32)


def block_levels(own_key, extent, cuts, low, top_value):
    def one(axis_at, blocks):
        heights = jax.random.uniform(jax.random.fold_in(jax.random.fold_in(own_key, 6), axis_at), (blocks,), jnp.float32, low / len(cuts), top_value / len(cuts))
        return jnp.repeat(jnp.exp(heights), extent[axis_at] // blocks).reshape((-1,) + (1,) * (len(extent) - axis_at - 1))

    loudness = one(*cuts[0])
    for cut in cuts[1:]:
        loudness = loudness * one(*cut)
    return loudness


def scatter_about(key, extent, spread, most, cuts=(), kind=jnp.bfloat16):
    gain = block_levels(key, extent, cuts, -0.22, 0.18) if cuts else 1.0
    array = jax.random.normal(key, extent, jnp.float32) * spread * gain
    return jnp.minimum(jnp.maximum(array, -most), most).astype(kind)


def setup_inputs(seed: int = 0) -> dict:
    key_of = jax.random.split(jax.random.key(seed), 16)
    activations = scatter_about(key_of[0], (SLOTS, SLOT_LEN, MODEL_WIDTH), 1.0, 6.0, ((0, 4), (1, 8)))
    cotangent = scatter_about(key_of[1], (SLOTS, SLOT_LEN, MODEL_WIDTH), 1.0, 6.0, ((0, 4), (1, 8)))
    norm_gains = jnp.clip(1.0 + 0.1 * jax.random.normal(key_of[2], (2, MODEL_WIDTH), jnp.float32), 0.5, 1.5)
    norm_shifts = scatter_about(key_of[3], (2, MODEL_WIDTH), 0.1, 0.6, (), jnp.float32)
    w_qkv = scatter_about(key_of[4], (MODEL_WIDTH, 3 * MODEL_WIDTH), MODEL_WIDTH ** -0.5, 0.1875)
    query_value_bias = scatter_about(key_of[5], (2, MODEL_WIDTH), 0.5, 3.0, (), jnp.float32)
    w_out = scatter_about(key_of[6], (MODEL_WIDTH, MODEL_WIDTH), (MODEL_WIDTH // 16) ** -0.5, 0.75)
    resid_bias = scatter_about(key_of[7], (2, MODEL_WIDTH), 0.2, 1.2, (), jnp.float32)
    w_fc = scatter_about(key_of[8], (MODEL_WIDTH, FF), MODEL_WIDTH ** -0.5, 0.1875)
    fc_bias = scatter_about(key_of[9], (FF,), 0.5, 3.0, (), jnp.float32)
    w_proj = scatter_about(key_of[10], (FF, MODEL_WIDTH), FF ** -0.5, 0.09375)
    doc_ids = draw_doc_ids(jax.random.fold_in(key_of[15], 71), 0)
    adapters = scatter_about(key_of[12], (4, RANK, MODEL_WIDTH), 0.05, 0.3, (), jnp.float32)
    moment_one = scatter_about(key_of[13], (4, RANK, MODEL_WIDTH), 1.0, 6.0, (), jnp.float32)
    moment_two = jnp.clip(jnp.exp(jax.random.uniform(key_of[14], (4, RANK, MODEL_WIDTH), jnp.float32, math.log(0.0002), math.log(0.004))), 0.0002, 0.004)
    return dict(activations=activations, cotangent=cotangent, norm_gains=norm_gains, norm_shifts=norm_shifts, w_qkv=w_qkv, query_value_bias=query_value_bias, w_out=w_out, resid_bias=resid_bias, w_fc=w_fc, fc_bias=fc_bias, w_proj=w_proj, doc_ids=doc_ids, adapters=adapters, moment_one=moment_one, moment_two=moment_two)


@jax.custom_vjp
def low_rank_rows(v):
    return lax.optimization_barrier(v.astype(jnp.bfloat16)).astype(jnp.float32)

@jax.custom_vjp
def low_rank_gradient(v):
    return v

def low_keep(v):
    return (low_rank_rows(v), None)

def low_pass(kept, grad):
    return (grad,)

def back_keep(v):
    return (v, None)

def back_low(kept, grad):
    return (low_rank_rows(grad),)
low_rank_rows.defvjp(low_keep, low_pass)
low_rank_gradient.defvjp(back_keep, back_low)
norm_floor = 1e-05
adapter_scale = 8.0
learn_rate = 0.005
beta_first = 0.9
beta_second = 0.999
adam_floor = 1e-08
decay_rate = 0.01
step_count = 100
masked_score = -1e+30

def matrix_product(left, right):
    return jnp.dot(left, right, precision=lax.Precision.HIGHEST)

def layer_norm(row_block, norm_gain, norm_shift):
    center = row_block - lax.optimization_barrier(jnp.mean(row_block, axis=-1, keepdims=True))
    scale_inv = lax.rsqrt(lax.optimization_barrier(jnp.mean(center * center, axis=-1, keepdims=True)) + norm_floor)
    return center * scale_inv * norm_gain + norm_shift

def attend_slot(pieces):
    query_matrix, key_rows, value_matrix, documents = pieces
    scores = jnp.einsum('qhd,khd->hqk', query_matrix, key_rows, precision=lax.Precision.HIGHEST) * 0.125
    scores = low_rank_gradient(scores)
    places = jnp.arange(SLOT_LEN, dtype=jnp.int32)
    allowed = (places[None, :] <= places[:, None]) & (documents[None, :] == documents[:, None])
    scores = jnp.where(allowed[None], scores, masked_score)
    highest = lax.optimization_barrier(jnp.max(scores, axis=-1, keepdims=True))
    weights = jnp.exp(scores - highest)
    chances = low_rank_rows(weights / lax.optimization_barrier(jnp.sum(weights, axis=-1, keepdims=True)))
    return jnp.einsum('hqk,khd->qhd', chances, value_matrix, precision=lax.Precision.HIGHEST)

def forward(slab_in, adapter_in, frozen, documents):
    norm_gains, norm_shifts, w_qkv, query_value_bias, w_out, resid_bias, w_fc, fc_bias, w_proj = frozen
    slot_count = slab_in.shape[0]
    row_block = slab_in.reshape(slot_count * SLOT_LEN, MODEL_WIDTH)
    normed_one = low_rank_rows(layer_norm(row_block, norm_gains[0], norm_shifts[0]))
    rounded_result = low_rank_rows(adapter_in)
    projected_rows = matrix_product(normed_one, w_qkv)
    query_down_output = low_rank_gradient(low_rank_rows(matrix_product(normed_one, rounded_result[0].T)))
    value_down_output = low_rank_gradient(low_rank_rows(matrix_product(normed_one, rounded_result[2].T)))
    query_matrix = low_rank_gradient(low_rank_rows(projected_rows[:, :MODEL_WIDTH] + query_value_bias[0] + adapter_scale * matrix_product(query_down_output, rounded_result[1])))
    key_rows = low_rank_gradient(low_rank_rows(projected_rows[:, MODEL_WIDTH:2 * MODEL_WIDTH]))
    value_matrix = low_rank_gradient(low_rank_rows(projected_rows[:, 2 * MODEL_WIDTH:] + query_value_bias[1] + adapter_scale * matrix_product(value_down_output, rounded_result[3])))
    head_shape = (slot_count, SLOT_LEN, HEADS, HEAD_DIM)
    attended = lax.map(jax.checkpoint(attend_slot), (query_matrix.reshape(head_shape), key_rows.reshape(head_shape), value_matrix.reshape(head_shape), documents))
    attended = low_rank_gradient(low_rank_rows(attended.reshape(slot_count * SLOT_LEN, MODEL_WIDTH)))
    branch = low_rank_gradient(matrix_product(attended, w_out) + resid_bias[0])
    middle = row_block + branch
    normed_two = low_rank_rows(layer_norm(middle, norm_gains[1], norm_shifts[1]))
    hidden = low_rank_gradient(matrix_product(normed_two, w_fc) + fc_bias)
    active = low_rank_rows(jax.nn.gelu(hidden, approximate=True))
    result = middle + matrix_product(active, w_proj) + resid_bias[1]
    return result.reshape(slot_count, SLOT_LEN, MODEL_WIDTH)

def reference(activations, cotangent, norm_gains, norm_shifts, w_qkv, query_value_bias, w_out, resid_bias, w_fc, fc_bias, w_proj, doc_ids, adapters, moment_one, moment_two):
    frozen = tuple((member.astype(jnp.float32) for member in (norm_gains, norm_shifts, w_qkv, query_value_bias, w_out, resid_bias, w_fc, fc_bias, w_proj)))
    per_group = 4
    group_count = SLOTS // per_group
    slab_groups = activations.astype(jnp.float32).reshape(group_count, per_group, SLOT_LEN, MODEL_WIDTH)
    pull_groups = cotangent.astype(jnp.float32).reshape(group_count, per_group, SLOT_LEN, MODEL_WIDTH)
    doc_groups = doc_ids.reshape(group_count, per_group, SLOT_LEN)

    def group_step(running, inputs):
        slab_in, pull_in, group_docs = inputs

        def apply_block(slab_arg, adapter_arg):
            return forward(slab_arg, adapter_arg, frozen, group_docs)
        result, backward = jax.vjp(apply_block, slab_in, adapters)
        grad_slab, grad_adapters = backward(pull_in)
        return (running + grad_adapters, (result.astype(jnp.bfloat16), grad_slab.astype(jnp.bfloat16)))
    adapter_grads, (outputs, input_grads) = lax.scan(group_step, jnp.zeros_like(adapters), (slab_groups, pull_groups, doc_groups))
    block_output = outputs.reshape(SLOTS, SLOT_LEN, MODEL_WIDTH)
    input_grad = input_grads.reshape(SLOTS, SLOT_LEN, MODEL_WIDTH)
    norm_total = jnp.sqrt(jnp.sum(adapter_grads * adapter_grads))
    clipped_grads = adapter_grads * jnp.minimum(1.0, math.sqrt(4.0 * RANK * MODEL_WIDTH) / norm_total)
    new_moment_one = beta_first * moment_one + (1.0 - beta_first) * clipped_grads
    new_moment_two = beta_second * moment_two + (1.0 - beta_second) * clipped_grads * clipped_grads
    first_hat = new_moment_one / (1.0 - beta_first ** step_count)
    second_hat = new_moment_two / (1.0 - beta_second ** step_count)
    new_adapters = adapters - learn_rate * (first_hat / (jnp.sqrt(second_hat) + adam_floor) + decay_rate * adapters)
    return (block_output, input_grad, clipped_grads, new_adapters, new_moment_one, new_moment_two)
```

```python
from functools import partial
import math

import jax
import jax.numpy as jnp
from jax import lax
from jax.experimental import pallas as pl
from jax.experimental.pallas import tpu as pltpu
from jax.sharding import PartitionSpec as P

WIDTH = 1024
HEADS = 16
HEAD_DIM = 64
RANK = 4
LAYERS = 4
PAIRS = HEADS // 2
PAIR = 2 * HEAD_DIM
LOW = 128
LOW_V = 8
VROWS = PAIR + 16

norm_floor = 1e-05
adapter_scale = 8.0
learn_rate = 0.005
beta_first = 0.9
beta_second = 0.999
adam_floor = 1e-08
decay_rate = 0.01
step_count = 100
masked_score = -1e30

F32 = jnp.float32
BF16 = jnp.bfloat16
GELU_C = math.sqrt(2.0 / math.pi)
VMEM_BYTES = 60 * 2**20


def dot(left, right):
    return jnp.dot(left, right, preferred_element_type=F32)


def dot_t(left, right):
    return lax.dot_general(left, right, (((1,), (1,)), ((), ())), preferred_element_type=F32)


def norm_parts(rows):
    center = rows - jnp.mean(rows, axis=-1, keepdims=True)
    scale_inv = lax.rsqrt(jnp.mean(center * center, axis=-1, keepdims=True) + norm_floor)
    return center * scale_inv, scale_inv


def norm_back(grad_out, standard, scale_inv, gain):
    scaled = grad_out * gain
    return scale_inv * (
        scaled
        - jnp.mean(scaled, axis=-1, keepdims=True)
        - standard * jnp.mean(scaled * standard, axis=-1, keepdims=True)
    )


def gelu_parts(hidden):
    square = hidden * hidden
    bend = jnp.tanh(hidden * (GELU_C + (GELU_C * 0.044715) * square))
    half = 0.5 + 0.5 * bend
    slope = half + hidden * (1.0 - bend * bend) * (0.5 * GELU_C + (1.5 * GELU_C * 0.044715) * square)
    return hidden * half, slope


def block_start(layer):
    return layer * (layer + 1) // 2


def fill_bias(spot, docs, bias, shard, span):
    own, member = spot[0], spot[1]
    for layer in range(LAYERS):
        row = docs[own ^ layer]
        starts = jnp.concatenate([row, row], axis=1)
        keys = span * (layer + 1)
        key_at = lax.broadcasted_iota(jnp.int32, (keys, 2 * shard), 0)
        query_at = lax.broadcasted_iota(jnp.int32, (1, 2 * shard), 1)
        query_at = jnp.where(query_at >= shard, query_at - shard, query_at)
        query_at = query_at + (layer * span + member * shard)
        allowed = (key_at >= starts) & (key_at <= query_at)
        bias[pl.ds(block_start(layer) * span, keys), :] = jnp.where(allowed, 0.0, masked_score)


def spread(block, shard):
    none = jnp.zeros((HEAD_DIM, shard), block.dtype)
    return jnp.concatenate(
        [
            jnp.concatenate([block[:HEAD_DIM], none], axis=1),
            jnp.concatenate([none, block[HEAD_DIM:]], axis=1),
        ],
        axis=0,
    )


def gather_diagonal(block, shard):
    return jnp.concatenate([block[:HEAD_DIM, :shard], block[HEAD_DIM:PAIR, shard:]], axis=0)


def pipelined(tasks, first, second, third):
    ready = first(*tasks[0])
    waiting = None
    for place, task in enumerate(tasks):
        following = first(*tasks[place + 1]) if place + 1 < len(tasks) else None
        weighed = second(*task, *ready)
        if waiting is not None:
            third(*waiting)
        waiting = (*task, *weighed)
        ready = following
    third(*waiting)


def rows_of(message, shard):
    parts = [message[part * shard : (part + 1) * shard, :] for part in range(WIDTH // 128)]
    return jnp.concatenate(parts, axis=1).astype(F32)


def forward_kernel(group, shard, spot, gains, shifts, qv_bias, resid, fc_bias, low, up_q, up_v, *refs):
    pieces, refs = refs[: LAYERS * group], refs[LAYERS * group :]
    wqkv_h, wout_h, wfc_h, wproj_h = refs[:4]
    out_h, refs = refs[4 : 4 + LAYERS], refs[4 + LAYERS :]
    keys_h, values_h, spread_h, attended_h, middle_h, slope_h, log_total, docs = refs[:8]
    x, normed, keys, values, values_t, query, spread_q, bias, attended_t, attended = refs[8:18]
    middle, normed_two, active, slope, out, wbuf, wout, wproj = refs[18:26]
    in_sem, w_sem, out_sem = refs[26:]
    span = group * shard
    rows = LAYERS * shard
    width_fc = wfc_h.shape[1]
    own, member = spot[0], spot[1]

    loads = [
        pltpu.make_async_copy(pieces[place], x.at[place], in_sem.at[place]) for place in range(LAYERS * group)
    ]
    for load in loads:
        load.start()
    load_qkv = pltpu.make_async_copy(wqkv_h, wbuf.at[:, pl.ds(0, 3 * WIDTH)], w_sem.at[0])
    load_qkv.start()
    load_out = pltpu.make_async_copy(wout_h, wout, w_sem.at[1])
    load_out.start()
    load_proj = pltpu.make_async_copy(wproj_h, wproj, w_sem.at[2])
    load_proj.start()
    load_fc = pltpu.make_async_copy(wfc_h, wbuf, w_sem.at[3])
    for turn in range(LAYERS):
        for other in range(group):
            place = turn * group + other
            loads[place].wait()
            if other == 0:
                numbers = x[place, WIDTH // 128 * shard :, :].astype(F32)
                docs[turn] = (numbers[0:1, :shard] * 32.0 + numbers[1:2, :shard]).astype(jnp.int32)
            standard, _ = norm_parts(rows_of(x.at[place], shard))
            at = pl.ds(pl.multiple_of((own ^ turn) * span + (member ^ other) * shard, shard), shard)
            normed[at, :] = (standard * gains[0:1, :] + shifts[0:1, :]).astype(BF16)
    fill_bias(spot, docs, bias, shard, span)
    load_qkv.wait()
    low_rows = dot_t(normed[...], low[...]).astype(BF16)
    half = WIDTH // 2
    for first in range(0, WIDTH, half):
        at = pl.ds(first, half)
        keys[:, at] = dot(normed[...], wbuf[:, WIDTH + first : WIDTH + first + half]).astype(BF16)
    for first in range(0, WIDTH, half):
        at = pl.ds(first, half)
        values[:, at] = (
            dot(normed[...], wbuf[:, 2 * WIDTH + first : 2 * WIDTH + first + half])
            + qv_bias[1:2, at]
            + dot(low_rows, up_v[:, at])
        ).astype(BF16)
    mine = jnp.concatenate(
        [normed[pl.ds(pl.multiple_of(layer * span + member * shard, shard), shard), :] for layer in range(LAYERS)],
        axis=0,
    )
    low_mine = dot_t(mine, low[...]).astype(BF16)
    query[...] = (
        (dot(mine, wbuf[:, :WIDTH]) + qv_bias[0:1, :] + dot(low_mine, up_q[...])).astype(BF16) * 0.125
    ).astype(BF16)
    load_fc.start()
    stores = [
        pltpu.make_async_copy(keys, keys_h, out_sem.at[0]),
        pltpu.make_async_copy(values, values_h, out_sem.at[1]),
    ]
    for store in stores:
        store.start()

    def attend(step, _):
        both = []
        for side in range(2):
            at = pl.ds(pl.multiple_of((2 * step + side) * PAIR, PAIR), PAIR)
            values_t[side, :PAIR, :] = values[:, at].T
            values_t[side, PAIR:, :] = jnp.ones((VROWS - PAIR, values.shape[0]), BF16)
            for layer in range(LAYERS):
                block = query[layer * shard : (layer + 1) * shard, at].T
                spread_q[at, layer * 2 * shard : (layer + 1) * 2 * shard] = spread(block, shard)
            both.append(at)

        def score(side, layer):
            seen = span * (layer + 1)
            scores = dot(keys[0:seen, both[side]], spread_q[both[side], layer * 2 * shard : (layer + 1) * 2 * shard])
            return (scores + bias[block_start(layer) * span : block_start(layer) * span + seen, :],)

        def weigh(side, layer, scores):
            highest = jnp.max(scores, axis=0, keepdims=True)
            return highest, jnp.exp(scores - highest).astype(BF16)

        def gather(side, layer, highest, weights):
            seen = span * (layer + 1)
            summed = dot(values_t[side, :, 0:seen], weights)
            totals = summed[PAIR : PAIR + 1, :]
            block = gather_diagonal(summed[:PAIR] * (1.0 / totals), shard)
            attended_t[both[side], layer * shard : (layer + 1) * shard] = block
            at = pl.ds(pl.multiple_of((own ^ layer) * shard, shard), shard)
            attended[at, both[side]] = block.T.astype(BF16)
            log_total[2 * step + side, layer : layer + 1, :] = highest + jnp.log(totals)

        tasks = [(side, layer) for side in range(2) for layer in range(LAYERS)]
        pipelined(tasks, score, weigh, gather)
        return 0

    lax.fori_loop(0, PAIRS // 2, attend, 0)
    stores.append(pltpu.make_async_copy(spread_q, spread_h, out_sem.at[2]))
    stores.append(pltpu.make_async_copy(attended_t, attended_h, out_sem.at[3]))
    for store in stores[2:]:
        store.start()
    load_out.wait()
    branch = dot(attended[...], wout[...]) + resid[0:1, :]
    for turn in range(LAYERS):
        at = pl.ds(turn * shard, shard)
        center = rows_of(x.at[turn * group], shard) + branch[turn * shard : (turn + 1) * shard]
        middle[at, :] = center
        standard, _ = norm_parts(center)
        normed_two[at, :] = (standard * gains[1:2, :] + shifts[1:2, :]).astype(BF16)
    stores.append(pltpu.make_async_copy(middle, middle_h, out_sem.at[4]))
    stores[-1].start()
    load_fc.wait()
    chunk = 1024
    for first in range(0, width_fc, chunk):
        at = pl.ds(first, chunk)
        act, tilt = gelu_parts(dot(normed_two[...], wbuf[:, at]) + fc_bias[:, at])
        active[:, at] = act.astype(BF16)
        slope[:, at] = tilt.astype(BF16)
    stores.append(pltpu.make_async_copy(slope, slope_h, out_sem.at[5]))
    stores[-1].start()
    load_proj.wait()
    for first in range(0, WIDTH, half):
        at = pl.ds(first, half)
        out[:, at] = (middle[:, at] + dot(active[...], wproj[:, at]) + resid[1:2, at]).astype(BF16)
    for turn in range(LAYERS):
        stores.append(
            pltpu.make_async_copy(out.at[pl.ds(turn * shard, shard), :], out_h[turn], out_sem.at[6 + turn])
        )
        stores[-1].start()
    for store in stores:
        store.wait()


def backward_kernel(group, shard, spot, docs, gains, log_total, *refs):
    pulls = refs[:LAYERS]
    slope_h, middle_h, keys_h, values_h, spread_h, attended_h, wproj_h, wfc_h, wout_h = refs[LAYERS : LAYERS + 9]
    refs = refs[LAYERS + 9 :]
    gm_h, dq_h, refs = refs[0], refs[1], refs[2:]
    pair_h, refs = refs[:group], refs[group:]
    pull, slope, grad_hidden, gn, middle, grad_att, keys, values, spread_q, attended_t = refs[:10]
    bias, keys_t, spread_g, dq, dq_t, dk, dv, wproj, wfc, wout = refs[10:20]
    in_sem, out_sem = refs[20:]
    span = group * shard
    rows = LAYERS * shard
    length = LAYERS * span
    width_fc = wfc_h.shape[1]
    chunk = 1024
    own, member = spot[0], spot[1]

    load_pull = [
        pltpu.make_async_copy(pulls[turn], pull.at[pl.ds(turn * shard, shard), :], in_sem.at[turn])
        for turn in range(LAYERS)
    ]
    load_proj, load_slope = [], []
    for part in range(width_fc // chunk):
        at = pl.ds(part * chunk, chunk)
        load_proj.append(pltpu.make_async_copy(wproj_h.at[at, :], wproj.at[at, :], in_sem.at[LAYERS + 2 * part]))
        load_slope.append(
            pltpu.make_async_copy(slope_h.at[:, at], slope.at[:, at], in_sem.at[LAYERS + 2 * part + 1])
        )
    base = LAYERS + 2 * (width_fc // chunk)
    load_rest = [
        pltpu.make_async_copy(source, target, in_sem.at[base + place])
        for place, (source, target) in enumerate(
            (
                (wfc_h, wfc),
                (middle_h, middle),
                (wout_h, wout),
                (keys_h, keys),
                (values_h, values),
                (spread_h, spread_q),
                (attended_h, attended_t),
            )
        )
    ]
    for load in load_pull:
        load.start()
    for one, two in zip(load_proj, load_slope):
        one.start()
        two.start()
    for load in load_rest:
        load.start()
    fill_bias(spot, docs, bias, shard, span)
    for load in load_pull:
        load.wait()
    for part in range(width_fc // chunk):
        at = pl.ds(part * chunk, chunk)
        load_proj[part].wait()
        load_slope[part].wait()
        grad_hidden[:, at] = (dot_t(pull[...], wproj[at, :]) * slope[:, at].astype(F32)).astype(BF16)
    load_rest[0].wait()
    half = WIDTH // 2
    for first in range(0, WIDTH, half):
        at = pl.ds(first, half)
        gn[:, at] = dot_t(grad_hidden[...], wfc[at, :])
    load_rest[1].wait()
    load_rest[2].wait()
    standard, scale_inv = norm_parts(middle[...])
    grad_middle = pull[...].astype(F32) + norm_back(gn[...], standard, scale_inv, gains[1:2, :])
    gn[...] = grad_middle
    stores = [pltpu.make_async_copy(gn, gm_h, out_sem.at[0])]
    stores[0].start()
    grad_att[...] = dot_t(grad_middle.astype(BF16), wout[...]).astype(BF16)
    for load in load_rest[3:]:
        load.wait()

    def attend(step, _):
        both = [pl.ds(pl.multiple_of((2 * step + side) * PAIR, PAIR), PAIR) for side in range(2)]
        for side in range(2):
            keys_t[side] = keys[:, both[side]].T
        deltas = {}
        totals = {}

        def score(side, layer, first):
            cut = pl.ds(layer * 2 * shard, 2 * shard)
            if first == 0:
                at = pl.ds(pl.multiple_of((own ^ layer) * shard, shard), shard)
                block = grad_att[at, both[side]].T
                product = block.astype(F32) * attended_t[both[side], layer * shard : (layer + 1) * shard]
                deltas[side, layer] = jnp.concatenate(
                    [
                        jnp.sum(product[:HEAD_DIM], axis=0, keepdims=True),
                        jnp.sum(product[HEAD_DIM:], axis=0, keepdims=True),
                    ],
                    axis=1,
                )
                spread_g[side, :, layer * 2 * shard : (layer + 1) * 2 * shard] = spread(block, shard)
            key_rows = keys[first : first + span, both[side]]
            value_rows = values[first : first + span, both[side]]
            start = block_start(layer) * span + first
            scores = dot(key_rows, spread_q[both[side], cut]) + bias[start : start + span, :]
            return scores, dot(value_rows, spread_g[side, :, cut])

        def weigh(side, layer, first, scores, grad_chances):
            chances = jnp.exp(scores - log_total[2 * step + side, layer : layer + 1, :])
            grad_scores = chances * (grad_chances - deltas[side, layer])
            return chances.astype(BF16), grad_scores.astype(BF16)

        def gather(side, layer, first, chances, grad_scores):
            cut = pl.ds(layer * 2 * shard, 2 * shard)
            back_v = dot_t(spread_g[side, :, cut], chances)
            back_k = dot_t(spread_q[both[side], cut], grad_scores)
            back_q = dot(keys_t[side, :, first : first + span], grad_scores)
            part = first // span
            if layer == part:
                totals[side, part] = (back_k, back_v)
            else:
                before = totals[side, part]
                totals[side, part] = (before[0] + back_k, before[1] + back_v)
            if first > 0:
                back_q = back_q + dq_t[side]
            if layer == part:
                at = pl.ds(pl.multiple_of((own ^ layer) * shard, shard), shard)
                dq[at, both[side]] = (gather_diagonal(back_q, shard) * 0.125).T.astype(BF16)
            else:
                dq_t[side] = back_q
            if layer == LAYERS - 1:
                done_k, done_v = totals.pop((side, part))
                dk[first : first + span, both[side]] = done_k.T.astype(BF16)
                dv[first : first + span, both[side]] = done_v.T.astype(BF16)

        tasks = [
            (side, layer, part * span) for side in range(2) for layer in range(LAYERS) for part in range(layer + 1)
        ]
        pipelined(tasks, score, weigh, gather)
        return 0

    lax.fori_loop(0, PAIRS // 2, attend, 0)
    stores.append(pltpu.make_async_copy(dq, dq_h, out_sem.at[1]))
    stores[-1].start()
    count = 2
    for other in range(group - 1, -1, -1):
        for turn in range(LAYERS):
            at = pl.ds(pl.multiple_of((own ^ turn) * span + (member ^ other) * shard, shard), shard)
            to = pl.ds(turn * shard, shard)
            for place, source in enumerate((dk, dv)):
                stores.append(
                    pltpu.make_async_copy(
                        source.at[at, :],
                        pair_h[other].at[to, pl.ds(place * WIDTH, WIDTH)],
                        out_sem.at[count],
                    )
                )
                stores[-1].start()
                count += 1
    for store in stores:
        store.wait()


def closing_kernel(group, shard, gains, shifts, low, up_q, up_v, *refs):
    pieces, refs = refs[:LAYERS], refs[LAYERS:]
    gm_h, dq_h, wqkv_h = refs[:3]
    pair_h, refs = refs[3 : 3 + group], refs[3 + group :]
    grads, terms, refs = refs[:LAYERS], refs[LAYERS], refs[LAYERS + 1 :]
    x, gm, stack, pairs, wqkv, normed, sem = refs
    loads = [
        pltpu.make_async_copy(pieces[turn], x.at[turn], sem.at[turn]) for turn in range(LAYERS)
    ]
    loads.append(pltpu.make_async_copy(dq_h, stack.at[:, pl.ds(0, WIDTH)], sem.at[LAYERS]))
    for other in range(group):
        loads.append(pltpu.make_async_copy(pair_h[other], pairs.at[other], sem.at[LAYERS + 1 + other]))
    loads.append(pltpu.make_async_copy(gm_h, gm, sem.at[LAYERS + 1 + group]))
    load_w = pltpu.make_async_copy(wqkv_h, wqkv, sem.at[LAYERS + 2 + group])
    for load in loads:
        load.start()
    load_w.start()
    for load in loads[:LAYERS]:
        load.wait()
    whole = jnp.concatenate([rows_of(x.at[turn], shard) for turn in range(LAYERS)], axis=0)
    standard, scale_inv = norm_parts(whole)
    normed[...] = (standard * gains[0:1, :] + shifts[0:1, :]).astype(BF16)
    low_rows = dot_t(normed[...], low[...]).astype(BF16)
    for load in loads[LAYERS:]:
        load.wait()
    total = pairs[0].astype(F32)
    for other in range(1, group):
        total = total + pairs[other].astype(F32)
    stack[:, WIDTH:] = total.astype(BF16)
    down = (dot_t(stack[:, :WIDTH], up_q[...]) + dot_t(stack[:, 2 * WIDTH :], up_v[...])).astype(BF16)
    load_w.wait()
    grad_normed = dot_t(stack[...], wqkv[...]) + dot(down, low[...])
    grad_rows = gm[...] + norm_back(grad_normed, standard, scale_inv, gains[0:1, :])
    for turn in range(LAYERS):
        grads[turn][...] = grad_rows[turn * shard : (turn + 1) * shard].astype(BF16)
    down_t = down.T[:16]
    low_t = low_rows.T[:16]
    first = dot(down_t, normed[...])
    second = dot(low_t, stack[:, :WIDTH])
    third = dot(low_t, stack[:, 2 * WIDTH :])
    terms[0] = first[:RANK]
    terms[1] = adapter_scale * second[:RANK]
    terms[2] = first[LOW_V : LOW_V + RANK]
    terms[3] = adapter_scale * third[LOW_V : LOW_V + RANK]


def place_kernel(spot, *refs):
    pieces, whole = refs[:LAYERS], refs[LAYERS]
    for turn in range(LAYERS):
        whole[spot[0] ^ turn] = pieces[turn][...]


def pack_kernel(shard, spot, docs, whole, *messages):
    for turn in range(LAYERS):
        slot = spot[0] ^ turn
        for part in range(WIDTH // 128):
            messages[turn][part * shard : (part + 1) * shard, :] = whole[slot, :, part * 128 : (part + 1) * 128]
        row = docs[pl.ds(slot, 1), :]
        high = row >> 5
        both = jnp.concatenate([high, row - (high << 5)], axis=0).astype(F32)
        if shard < 128:
            both = jnp.concatenate([both, jnp.zeros((2, 128 - shard), F32)], axis=1)
        both = jnp.concatenate([both, jnp.zeros((14, 128), F32)], axis=0)
        messages[turn][WIDTH // 128 * shard :, :] = both.astype(BF16)


def cut_kernel(spot, whole, *pieces):
    for turn in range(LAYERS):
        pieces[turn][...] = whole[spot[0] ^ turn]


def adam_update(adapter_grads, adapters, moment_one, moment_two):
    norm_total = jnp.sqrt(jnp.sum(adapter_grads * adapter_grads))
    clipped_grads = adapter_grads * jnp.minimum(1.0, math.sqrt(4.0 * RANK * WIDTH) / norm_total)
    new_moment_one = beta_first * moment_one + (1.0 - beta_first) * clipped_grads
    new_moment_two = beta_second * moment_two + (1.0 - beta_second) * clipped_grads * clipped_grads
    first_hat = new_moment_one / (1.0 - beta_first**step_count)
    second_hat = new_moment_two / (1.0 - beta_second**step_count)
    new_adapters = adapters - learn_rate * (
        first_hat / (jnp.sqrt(second_hat) + adam_floor) + decay_rate * adapters
    )
    return (clipped_grads, new_adapters, new_moment_one, new_moment_two)


VM = pl.BlockSpec(memory_space=pltpu.VMEM)
SM = pl.BlockSpec(memory_space=pltpu.SMEM)
ANY = pl.BlockSpec(memory_space=pl.ANY)


def shaped(dtype, *shape):
    return jax.ShapeDtypeStruct(shape, dtype)


class Routes:
    def __init__(self, slots, blks):
        self.slots, self.blks = slots, blks
        self.group = blks // LAYERS
        self.chips = self.group // 2

    def gathering(self, turn):
        pairs = []
        for slot in range(self.slots):
            for blk in range(self.blks):
                layer, member = blk // self.group, blk % self.group
                target = (2 * (layer ^ turn) + slot % 2) * self.chips + member // 2
                pairs.append((slot * self.blks + blk, (slot - slot % 2 + member % 2) * self.blks + target))
        return pairs

    def returning(self, turn):
        return [(target, source) for source, target in self.gathering(turn)]

    def within(self, other):
        pairs = []
        for slot in range(self.slots):
            for blk in range(self.blks):
                to_slot, to_blk = slot ^ (other & 1), blk ^ (other >> 1)
                pairs.append((slot * self.blks + blk, to_slot * self.blks + to_blk))
        return pairs

    def spot(self, slot, blk):
        own = blk // self.chips // 2
        member = (blk % self.chips) * 2 + slot % 2
        return own, member


def body(
    routes,
    activations,
    cotangent,
    norm_gains,
    norm_shifts,
    w_qkv,
    query_value_bias,
    w_out,
    resid_bias,
    w_fc,
    fc_bias,
    w_proj,
    doc_ids,
    adapters,
    moment_one,
    moment_two,
):
    axes = ("slot", "blk")
    group = routes.group
    shard = activations.shape[1]
    span, rows, length = group * shard, LAYERS * shard, LAYERS * group * shard
    width_fc = w_fc.shape[1]
    slot, blk = lax.axis_index("slot"), lax.axis_index("blk")
    home = blk // group
    own, member = routes.spot(slot, blk)
    spot = jnp.stack([own, member]).astype(jnp.int32)
    home_spot = jnp.reshape(home, (1,)).astype(jnp.int32)
    turns = range(LAYERS)

    def pick(whole, turn):
        return lax.dynamic_index_in_dim(whole, home ^ turn, 0, keepdims=False)

    def send(piece, pairs):
        return lax.ppermute(piece, axes, pairs)

    params = pltpu.CompilerParams(vmem_limit_bytes=VMEM_BYTES)
    piece_shape = shaped(BF16, shard, WIDTH)
    message_rows = WIDTH // 128 * shard + 16

    messages = pl.pallas_call(
        partial(pack_kernel, shard),
        in_specs=[SM, VM, VM],
        out_specs=[VM] * LAYERS,
        out_shape=[shaped(BF16, message_rows, 128)] * LAYERS,
        name="pack",
    )(home_spot, doc_ids, activations)
    x_own = [None] * LAYERS
    for turn in (3, 2, 1, 0):
        x_own[turn] = send(messages[turn], routes.gathering(turn))
    pieces = []
    for turn in turns:
        pieces.append(x_own[turn])
        for other in range(1, group):
            pieces.append(send(x_own[turn], routes.within(other)))
    cuts = pl.pallas_call(
        cut_kernel,
        in_specs=[SM, VM],
        out_specs=[VM] * LAYERS,
        out_shape=[piece_shape] * LAYERS,
        name="cut",
    )(home_spot, cotangent)
    tied = lax.optimization_barrier((x_own[2], x_own[3], cuts))
    pulls = [send((cuts if turn < 2 else tied[2])[turn], routes.gathering(turn)) for turn in turns]

    rounded = adapters.astype(BF16)
    low = jnp.zeros((LOW, WIDTH), BF16).at[0:RANK].set(rounded[0]).at[LOW_V : LOW_V + RANK].set(rounded[2])
    eight = jnp.asarray(adapter_scale, BF16)
    up_q = jnp.zeros((LOW, WIDTH), BF16).at[0:RANK].set(rounded[1] * eight)
    up_v = jnp.zeros((LOW, WIDTH), BF16).at[LOW_V : LOW_V + RANK].set(rounded[3] * eight)

    forward = pl.pallas_call(
        partial(forward_kernel, group, shard),
        in_specs=[SM] + [VM] * 8 + [ANY] * (LAYERS * group + 4),
        out_specs=[ANY] * (LAYERS + 6) + [VM] * 2,
        out_shape=[piece_shape] * LAYERS
        + [
            shaped(BF16, length, WIDTH),
            shaped(BF16, length, WIDTH),
            shaped(BF16, WIDTH, 2 * rows),
            shaped(F32, WIDTH, rows),
            shaped(F32, rows, WIDTH),
            shaped(BF16, rows, width_fc),
            shaped(F32, PAIRS, LAYERS, 2 * shard),
            shaped(jnp.int32, LAYERS, 1, shard),
        ],
        scratch_shapes=[
            pltpu.VMEM((LAYERS * group, message_rows, 128), BF16),
            pltpu.VMEM((length, WIDTH), BF16),
            pltpu.VMEM((length, WIDTH), BF16),
            pltpu.VMEM((length, WIDTH), BF16),
            pltpu.VMEM((2, VROWS, length), BF16),
            pltpu.VMEM((rows, WIDTH), BF16),
            pltpu.VMEM((WIDTH, 2 * rows), BF16),
            pltpu.VMEM((block_start(LAYERS) * span, 2 * shard), F32),
            pltpu.VMEM((WIDTH, rows), F32),
            pltpu.VMEM((rows, WIDTH), BF16),
            pltpu.VMEM((rows, WIDTH), F32),
            pltpu.VMEM((rows, WIDTH), BF16),
            pltpu.VMEM((rows, width_fc), BF16),
            pltpu.VMEM((rows, width_fc), BF16),
            pltpu.VMEM((rows, WIDTH), BF16),
            pltpu.VMEM((WIDTH, width_fc), BF16),
            pltpu.VMEM((WIDTH, WIDTH), BF16),
            pltpu.VMEM((width_fc, WIDTH), BF16),
            pltpu.SemaphoreType.DMA((LAYERS * group,)),
            pltpu.SemaphoreType.DMA((4,)),
            pltpu.SemaphoreType.DMA((6 + LAYERS,)),
        ],
        compiler_params=params,
        cost_estimate=pl.CostEstimate(flops=22 * 10**9, bytes_accessed=40 * 2**20, transcendentals=0),
        name="forward",
    )
    results = forward(
        spot,
        norm_gains,
        norm_shifts,
        query_value_bias,
        resid_bias,
        fc_bias.reshape(1, width_fc),
        low,
        up_q,
        up_v,
        *pieces,
        w_qkv,
        w_out,
        w_fc,
        w_proj,
    )
    out_pieces = results[:LAYERS]
    keys, values, spread_q, attended_t, middle, slope, log_total, docs = results[LAYERS:]
    outs = [send(out_pieces[turn], routes.returning(turn)) for turn in turns]

    parts = width_fc // 1024
    backward = pl.pallas_call(
        partial(backward_kernel, group, shard),
        in_specs=[SM] + [VM] * 3 + [ANY] * (LAYERS + 9),
        out_specs=[ANY] * (2 + group),
        out_shape=[shaped(F32, rows, WIDTH), shaped(BF16, rows, WIDTH)]
        + [shaped(BF16, rows, 2 * WIDTH)] * group,
        scratch_shapes=[
            pltpu.VMEM((rows, WIDTH), BF16),
            pltpu.VMEM((rows, width_fc), BF16),
            pltpu.VMEM((rows, width_fc), BF16),
            pltpu.VMEM((rows, WIDTH), F32),
            pltpu.VMEM((rows, WIDTH), F32),
            pltpu.VMEM((rows, WIDTH), BF16),
            pltpu.VMEM((length, WIDTH), BF16),
            pltpu.VMEM((length, WIDTH), BF16),
            pltpu.VMEM((WIDTH, 2 * rows), BF16),
            pltpu.VMEM((WIDTH, rows), F32),
            pltpu.VMEM((block_start(LAYERS) * span, 2 * shard), F32),
            pltpu.VMEM((2, PAIR, length), BF16),
            pltpu.VMEM((2, PAIR, 2 * rows), BF16),
            pltpu.VMEM((rows, WIDTH), BF16),
            pltpu.VMEM((2, PAIR, 2 * shard), F32),
            pltpu.VMEM((length, WIDTH), BF16),
            pltpu.VMEM((length, WIDTH), BF16),
            pltpu.VMEM((width_fc, WIDTH), BF16),
            pltpu.VMEM((WIDTH, width_fc), BF16),
            pltpu.VMEM((WIDTH, WIDTH), BF16),
            pltpu.SemaphoreType.DMA((LAYERS + 2 * parts + 7,)),
            pltpu.SemaphoreType.DMA((2 + 2 * LAYERS * group,)),
        ],
        compiler_params=params,
        cost_estimate=pl.CostEstimate(flops=24 * 10**9, bytes_accessed=40 * 2**20, transcendentals=0),
        name="backward",
    )
    results = backward(
        spot,
        docs,
        norm_gains,
        log_total,
        *pulls,
        slope,
        middle,
        keys,
        values,
        spread_q,
        attended_t,
        w_proj,
        w_fc,
        w_out,
    )
    grad_middle, grad_query, grad_pairs = results[0], results[1], results[2:]
    received = [grad_pairs[0]] + [send(grad_pairs[other], routes.within(other)) for other in range(1, group)]

    outs, received = lax.optimization_barrier((outs, received))

    closing = pl.pallas_call(
        partial(closing_kernel, group, shard),
        in_specs=[VM] * 5 + [ANY] * (LAYERS + 3 + group),
        out_specs=[VM] * (LAYERS + 1),
        out_shape=[piece_shape] * LAYERS + [shaped(F32, 4, RANK, WIDTH)],
        scratch_shapes=[
            pltpu.VMEM((LAYERS, message_rows, 128), BF16),
            pltpu.VMEM((rows, WIDTH), F32),
            pltpu.VMEM((rows, 3 * WIDTH), BF16),
            pltpu.VMEM((group, rows, 2 * WIDTH), BF16),
            pltpu.VMEM((WIDTH, 3 * WIDTH), BF16),
            pltpu.VMEM((rows, WIDTH), BF16),
            pltpu.SemaphoreType.DMA((LAYERS + 3 + group,)),
        ],
        compiler_params=params,
        cost_estimate=pl.CostEstimate(flops=4 * 10**9, bytes_accessed=16 * 2**20, transcendentals=0),
        name="closing",
    )
    results = closing(
        norm_gains, norm_shifts, low, up_q, up_v, *x_own, grad_middle, grad_query, w_qkv, *received
    )
    grad_pieces, terms = results[:LAYERS], results[LAYERS]
    backs = [None] * LAYERS
    for turn in (3, 2, 1, 0):
        backs[turn] = send(grad_pieces[turn], routes.returning(turn))

    devices = routes.slots * routes.blks
    reach = 1
    while reach < devices:
        terms = terms + send(terms, [(device, device ^ reach) for device in range(devices)])
        reach *= 2
    clipped_grads, new_adapters, new_moment_one, new_moment_two = adam_update(
        terms, adapters, moment_one, moment_two
    )

    def assemble(home_pieces):
        return pl.pallas_call(
            place_kernel,
            in_specs=[SM] + [VM] * LAYERS,
            out_specs=VM,
            out_shape=shaped(BF16, LAYERS, shard, WIDTH),
            cost_estimate=pl.CostEstimate(flops=0, bytes_accessed=2 * 2**20, transcendentals=0),
            name="assemble",
        )(home_spot, *home_pieces)

    block_output = assemble(outs)
    input_grad = assemble(backs)
    return (block_output, input_grad, clipped_grads, new_adapters, new_moment_one, new_moment_two)


def solution(mesh):
    routes = Routes(mesh.shape["slot"], mesh.shape["blk"])
    rows = P("slot", "blk", None)
    placed = (rows, rows) + (P(),) * 9 + (P("slot", "blk"),) + (P(),) * 3
    return jax.shard_map(
        partial(body, routes),
        mesh=mesh,
        in_specs=placed,
        out_specs=(rows, rows, P(), P(), P(), P()),
        check_vma=False,
    )
```

```python
from functools import partial
import math

import jax
import jax.numpy as jnp
from jax import lax
from jax.experimental import pallas as pl
from jax.experimental.pallas import tpu as pltpu
from jax.sharding import PartitionSpec as P

WIDTH = 1024
HEADS = 16
HEAD_DIM = 64
RANK = 4
LAYERS = 4
PAIRS = HEADS // 2
PAIR = 2 * HEAD_DIM
LOW = 128
LOW_V = 8
NEAR = 2
VROWS = PAIR + 16

norm_floor = 1e-05
adapter_scale = 8.0
learn_rate = 0.005
beta_first = 0.9
beta_second = 0.999
adam_floor = 1e-08
decay_rate = 0.01
step_count = 100
masked_score = -1e30

F32 = jnp.float32
BF16 = jnp.bfloat16
GELU_C = math.sqrt(2.0 / math.pi)
VMEM_BYTES = 54 * 2**20
BACK_BYTES = 58 * 2**20
SMALL_BYTES = 59 * 2**20


def dot(left, right):
    return jnp.dot(left, right, preferred_element_type=F32)


def dot_t(left, right):
    return lax.dot_general(left, right, (((1,), (1,)), ((), ())), preferred_element_type=F32)


def norm_parts(rows):
    center = rows - jnp.mean(rows, axis=-1, keepdims=True)
    scale_inv = lax.rsqrt(jnp.mean(center * center, axis=-1, keepdims=True) + norm_floor)
    return center * scale_inv, scale_inv


def norm_back(grad_out, standard, scale_inv, gain):
    scaled = grad_out * gain
    return scale_inv * (
        scaled
        - jnp.mean(scaled, axis=-1, keepdims=True)
        - standard * jnp.mean(scaled * standard, axis=-1, keepdims=True)
    )


def gelu_parts(hidden):
    square = hidden * hidden
    bend = jnp.tanh(hidden * (GELU_C + (GELU_C * 0.044715) * square))
    half = 0.5 + 0.5 * bend
    slope = half + hidden * (1.0 - bend * bend) * (0.5 * GELU_C + (1.5 * GELU_C * 0.044715) * square)
    return hidden * half, slope


def block_start(layer):
    return layer * (layer + 1) // 2


def fill_bias(spot, docs, bias, shard, span):
    own, member = spot[1], spot[2]
    for layer in range(LAYERS):
        row = docs[own ^ layer]
        starts = jnp.concatenate([row, row], axis=1)
        keys = span * (layer + 1)
        key_at = lax.broadcasted_iota(jnp.int32, (keys, 2 * shard), 0)
        query_at = lax.broadcasted_iota(jnp.int32, (1, 2 * shard), 1)
        query_at = jnp.where(query_at >= shard, query_at - shard, query_at)
        query_at = query_at + (layer * span + member * shard)
        allowed = (key_at >= starts) & (key_at <= query_at)
        bias[pl.ds(block_start(layer) * span, keys), :] = jnp.where(allowed, 0.0, masked_score)


def spread(block, shard):
    none = jnp.zeros((HEAD_DIM, shard), block.dtype)
    return jnp.concatenate(
        [
            jnp.concatenate([block[:HEAD_DIM], none], axis=1),
            jnp.concatenate([none, block[HEAD_DIM:]], axis=1),
        ],
        axis=0,
    )


def gather_diagonal(block, shard):
    return jnp.concatenate([block[:HEAD_DIM, :shard], block[HEAD_DIM:PAIR, shard:]], axis=0)


def pipelined(tasks, first, second, third):
    ready = first(*tasks[0])
    waiting = None
    for place, task in enumerate(tasks):
        following = first(*tasks[place + 1]) if place + 1 < len(tasks) else None
        weighed = second(*task, *ready)
        if waiting is not None:
            third(*waiting)
        waiting = (*task, *weighed)
        ready = following
    third(*waiting)


def far_first(arrays, each=1):
    return [array for turn in range(LAYERS - 1, -1, -1) for array in arrays[turn * each : (turn + 1) * each]]


def rows_of(message, shard):
    parts = [message[part * shard : (part + 1) * shard, :] for part in range(WIDTH // 128)]
    return jnp.concatenate(parts, axis=1).astype(F32)


def forward_kernel(group, shard, spot, gains, shifts, qv_bias, resid, fc_bias, low, up_q, up_v, *refs):
    pieces, refs = far_first(refs[: LAYERS * group], group), refs[LAYERS * group :]
    wqkv_h, wout_h, wfc_h, wproj_h = refs[:4]
    out_h, refs = refs[4 : 4 + LAYERS], refs[4 + LAYERS :]
    keys_h, values_h, spread_h, attended_h, middle_h, slope_h, normed_h, log_total, docs = refs[:9]
    x, normed, keys, values, values_t, query, spread_q, bias, attended_t, attended = refs[9:19]
    middle, normed_two, total, slope, out, wbuf, wout, wproj = refs[19:27]
    in_sem, w_sem, out_sem = refs[27:]
    span = group * shard
    rows = LAYERS * shard
    width_fc = wfc_h.shape[1]
    own, member = spot[1], spot[2]

    loads = [
        pltpu.make_async_copy(pieces[place].at[pl.ds(0, x.shape[1]), :], x.at[place], in_sem.at[place])
        for place in range(LAYERS * group)
    ]
    for load in loads:
        load.start()
    load_qkv = []
    for place, part in enumerate((1, 2, 0)):
        at = pl.ds(part * WIDTH, WIDTH)
        load_qkv.append(pltpu.make_async_copy(wqkv_h.at[:, at], wbuf.at[pl.ds(0, WIDTH), at], w_sem.at[place]))
        load_qkv[-1].start()
    load_out = pltpu.make_async_copy(wout_h, wout, w_sem.at[3])
    load_fc = pltpu.make_async_copy(wfc_h, wbuf.at[pl.ds(0, WIDTH), :], w_sem.at[4])
    load_proj = pltpu.make_async_copy(wproj_h, wproj, w_sem.at[5])
    for turn in range(LAYERS):
        for other in range(group):
            place = turn * group + other
            loads[place].wait()
            if other == 0:
                numbers = x[place, WIDTH // 128 * shard :, :].astype(F32)
                docs[turn] = (numbers[0:1, :shard] * 32.0 + numbers[1:2, :shard]).astype(jnp.int32)
            standard, _ = norm_parts(rows_of(x.at[place], shard))
            at = pl.ds(pl.multiple_of((own ^ turn) * span + (member ^ other) * shard, shard), shard)
            normed[at, :WIDTH] = (standard * gains[0:1, :] + shifts[0:1, :]).astype(BF16)
    fill_bias(spot, docs, bias, shard, span)
    normed[:, WIDTH:] = dot_t(normed[:, :WIDTH], low[...]).astype(BF16)
    wbuf[WIDTH:, :WIDTH] = up_q[...]
    wbuf[WIDTH:, 2 * WIDTH : 3 * WIDTH] = up_v[...]
    half = WIDTH // 2
    load_qkv[0].wait()
    for first in range(0, WIDTH, half):
        at = pl.ds(first, half)
        keys[:, at] = dot(normed[:, :WIDTH], wbuf[:WIDTH, WIDTH + first : WIDTH + first + half]).astype(BF16)
    load_qkv[1].wait()
    for first in range(0, WIDTH, half):
        at = pl.ds(first, half)
        values[:, at] = (
            dot(normed[...], wbuf[:, 2 * WIDTH + first : 2 * WIDTH + first + half])
            + qv_bias[1:2, at]
        ).astype(BF16)
    own_rows = [pl.ds(pl.multiple_of(layer * span + member * shard, shard), shard) for layer in range(LAYERS)]
    mine = jnp.concatenate([normed[at, :] for at in own_rows], axis=0)
    load_qkv[2].wait()
    query[...] = (
        (dot(mine, wbuf[:, :WIDTH]) + qv_bias[0:1, :]).astype(BF16) * 0.125
    ).astype(BF16)
    load_out.start()
    load_fc.start()
    load_proj.start()
    stores = [
        pltpu.make_async_copy(keys, keys_h, out_sem.at[0]),
        pltpu.make_async_copy(values, values_h, out_sem.at[1]),
        pltpu.make_async_copy(normed, normed_h, out_sem.at[6 + LAYERS]),
    ]
    for store in stores:
        store.start()

    def attend(step, _):
        both = []
        for side in range(2):
            at = pl.ds(pl.multiple_of((2 * step + side) * PAIR, PAIR), PAIR)
            values_t[side, :PAIR, :] = values[:, at].T
            values_t[side, PAIR:, :] = jnp.ones((VROWS - PAIR, values.shape[0]), BF16)
            for layer in range(LAYERS):
                block = query[layer * shard : (layer + 1) * shard, at].T
                spread_q[at, layer * 2 * shard : (layer + 1) * 2 * shard] = spread(block, shard)
            both.append(at)

        def score(side, layer):
            seen = span * (layer + 1)
            scores = dot(keys[0:seen, both[side]], spread_q[both[side], layer * 2 * shard : (layer + 1) * 2 * shard])
            return (scores + bias[block_start(layer) * span : block_start(layer) * span + seen, :],)

        def weigh(side, layer, scores):
            highest = jnp.max(scores, axis=0, keepdims=True)
            return highest, jnp.exp(scores - highest).astype(BF16)

        def gather(side, layer, highest, weights):
            seen = span * (layer + 1)
            summed = dot(values_t[side, :, 0:seen], weights)
            totals = summed[PAIR : PAIR + 1, :]
            block = gather_diagonal(summed[:PAIR] * (1.0 / totals), shard)
            attended_t[both[side], layer * shard : (layer + 1) * shard] = block
            at = pl.ds(pl.multiple_of((own ^ layer) * shard, shard), shard)
            attended[at, both[side]] = block.T.astype(BF16)
            log_total[2 * step + side, layer : layer + 1, :] = highest + jnp.log(totals)

        tasks = [(side, layer) for side in range(2) for layer in range(LAYERS)]
        pipelined(tasks, score, weigh, gather)
        return 0

    lax.fori_loop(0, PAIRS // 2, attend, 0)
    stores.append(pltpu.make_async_copy(spread_q, spread_h, out_sem.at[2]))
    stores.append(pltpu.make_async_copy(attended_t, attended_h, out_sem.at[3]))
    for store in stores[3:]:
        store.start()
    load_out.wait()
    branch = dot(attended[...], wout[...]) + resid[0:1, :]
    for turn in range(LAYERS):
        at = pl.ds(turn * shard, shard)
        center = rows_of(x.at[turn * group], shard) + branch[turn * shard : (turn + 1) * shard]
        middle[at, :] = center
        standard, _ = norm_parts(center)
        normed_two[at, :] = (standard * gains[1:2, :] + shifts[1:2, :]).astype(BF16)
    stores.append(pltpu.make_async_copy(middle, middle_h, out_sem.at[4]))
    stores[-1].start()
    load_fc.wait()
    load_proj.wait()
    chunk = 1024
    hidden, acts = {}, {}
    count = width_fc // chunk
    for step in range(count + 2):
        if step < count:
            hidden[step] = dot(normed_two[...], wbuf[:WIDTH, step * chunk : (step + 1) * chunk])
        if 0 <= step - 1 < count:
            at = pl.ds((step - 1) * chunk, chunk)
            act, tilt = gelu_parts(hidden.pop(step - 1) + fc_bias[:, at])
            acts[step - 1] = act.astype(BF16)
            slope[:, at] = tilt.astype(BF16)
        if step == count:
            stores.append(pltpu.make_async_copy(slope, slope_h, out_sem.at[5]))
            stores[-1].start()
        if 0 <= step - 2:
            part = dot(acts.pop(step - 2), wproj[(step - 2) * chunk : (step - 1) * chunk, :])
            if step - 2 == 0:
                total[...] = part
            elif step - 1 < count:
                total[...] += part
            else:
                out[...] = (middle[...] + total[...] + part + resid[1:2, :]).astype(BF16)
    for turn in range(LAYERS):
        stores.append(
            pltpu.make_async_copy(out.at[pl.ds(turn * shard, shard), :], out_h[turn], out_sem.at[6 + turn])
        )
        stores[-1].start()
    for store in stores:
        store.wait()


def backward_kernel(group, shard, spot, docs, gains, log_total, low, up_q, up_v, *refs):
    pulls, refs = refs[:LAYERS], refs[LAYERS:]
    pieces, refs = refs[:LAYERS], refs[LAYERS:]
    slope_h, middle_h, spread_h, attended_h, wproj_h, wfc_h, wout_h, wqkv_h = refs[:8]
    keys_h, values_h, normed_h, refs = refs[8], refs[9], refs[10], refs[11:]
    gm_h, refs = refs[0], refs[1:]
    other_h, terms, refs = refs[: group - 1], refs[group - 1], refs[group:]
    pull, slope, grad_hidden, gn, middle, grad_att, keys, values, spread_q, attended_t = refs[:10]
    bias, keys_t, spread_g, dq, dq_t, dk, dv, wproj, wfc, wout, normed, messages = refs[10:22]
    in_sem, out_sem = refs[22:]
    span = group * shard
    rows = LAYERS * shard
    length = LAYERS * span
    width_fc = wfc_h.shape[1]
    chunk = 1024
    own, member = spot[1], spot[2]

    part_rows = WIDTH // 128 * shard
    load_pull = [
        pltpu.make_async_copy(
            pulls[turn], messages.at[turn], in_sem.at[turn]
        )
        for turn in range(LAYERS)
    ]
    load_proj, load_slope = [], []
    for part in range(width_fc // chunk):
        at = pl.ds(part * chunk, chunk)
        load_proj.append(pltpu.make_async_copy(wproj_h.at[at, :], wproj.at[at, :], in_sem.at[LAYERS + 2 * part]))
        load_slope.append(
            pltpu.make_async_copy(slope_h.at[:, at], slope.at[:, at], in_sem.at[LAYERS + 2 * part + 1])
        )
    base = LAYERS + 2 * (width_fc // chunk)
    load_rest = [
        pltpu.make_async_copy(source, target, in_sem.at[base + place])
        for place, (source, target) in enumerate(
            (
                (wfc_h, wfc),
                (middle_h, middle),
                (wout_h, wout),
                (keys_h, keys),
                (values_h, values),
                (spread_h, spread_q),
                (attended_h, attended_t),
                (normed_h, normed),
            )
        )
    ]
    for load in load_pull:
        load.start()
    for one, two in zip(load_proj, load_slope):
        one.start()
        two.start()
    for load in load_rest:
        load.start()
    fill_bias(spot, docs, bias, shard, span)
    for turn in range(LAYERS):
        load_pull[turn].wait()
        pull[turn * shard : (turn + 1) * shard, :] = rows_of(messages.at[turn], shard).astype(BF16)
    for part in range(width_fc // chunk):
        at = pl.ds(part * chunk, chunk)
        load_proj[part].wait()
        load_slope[part].wait()
        grad_hidden[:, at] = (dot_t(pull[...], wproj[at, :]) * slope[:, at].astype(F32)).astype(BF16)
    load_rest[0].wait()
    half = WIDTH // 2
    for first in range(0, WIDTH, half):
        at = pl.ds(first, half)
        gn[:, at] = dot_t(grad_hidden[...], wfc[at, :])
    load_rest[1].wait()
    load_rest[2].wait()
    standard, scale_inv = norm_parts(middle[...])
    grad_middle = pull[...].astype(F32) + norm_back(gn[...], standard, scale_inv, gains[1:2, :])
    gn[...] = grad_middle
    grad_att[...] = dot_t(grad_middle.astype(BF16), wout[...]).astype(BF16)
    load_last = [pltpu.make_async_copy(wqkv_h, wfc.at[:, pl.ds(0, 3 * WIDTH)], in_sem.at[base + len(load_rest)])]
    load_last.extend(
        pltpu.make_async_copy(pieces[turn].at[pl.ds(0, part_rows), :], messages.at[turn], in_sem.at[turn])
        for turn in range(LAYERS)
    )
    for load in load_last:
        load.start()
    for load in load_rest[3:]:
        load.wait()

    def attend(step, _):
        both = [pl.ds(pl.multiple_of((2 * step + side) * PAIR, PAIR), PAIR) for side in range(2)]
        for side in range(2):
            keys_t[side] = keys[:, both[side]].T
        deltas = {}
        totals = {}

        def score(side, layer, first):
            cut = pl.ds(layer * 2 * shard, 2 * shard)
            if first == 0:
                at = pl.ds(pl.multiple_of((own ^ layer) * shard, shard), shard)
                block = grad_att[at, both[side]].T
                product = block.astype(F32) * attended_t[both[side], layer * shard : (layer + 1) * shard]
                deltas[side, layer] = jnp.concatenate(
                    [
                        jnp.sum(product[:HEAD_DIM], axis=0, keepdims=True),
                        jnp.sum(product[HEAD_DIM:], axis=0, keepdims=True),
                    ],
                    axis=1,
                )
                spread_g[side, :, layer * 2 * shard : (layer + 1) * 2 * shard] = spread(block, shard)
            key_rows = keys[first : first + span, both[side]]
            value_rows = values[first : first + span, both[side]]
            start = block_start(layer) * span + first
            scores = dot(key_rows, spread_q[both[side], cut]) + bias[start : start + span, :]
            return scores, dot(value_rows, spread_g[side, :, cut])

        def weigh(side, layer, first, scores, grad_chances):
            chances = jnp.exp(scores - log_total[2 * step + side, layer : layer + 1, :])
            grad_scores = chances * (grad_chances - deltas[side, layer])
            return chances.astype(BF16), grad_scores.astype(BF16)

        def gather(side, layer, first, chances, grad_scores):
            cut = pl.ds(layer * 2 * shard, 2 * shard)
            back_v = dot_t(spread_g[side, :, cut], chances)
            back_k = dot_t(spread_q[both[side], cut], grad_scores)
            back_q = dot(keys_t[side, :, first : first + span], grad_scores)
            part = first // span
            if layer == part:
                totals[side, part] = (back_k, back_v)
            else:
                before = totals[side, part]
                totals[side, part] = (before[0] + back_k, before[1] + back_v)
            if first > 0:
                back_q = back_q + dq_t[side]
            if layer == part:
                at = pl.ds(pl.multiple_of((own ^ layer) * shard, shard), shard)
                dq[at, both[side]] = (gather_diagonal(back_q, shard) * 0.125).T.astype(BF16)
            else:
                dq_t[side] = back_q
            if layer == LAYERS - 1:
                done_k, done_v = totals.pop((side, part))
                dk[first : first + span, both[side]] = done_k.T.astype(BF16)
                dv[first : first + span, both[side]] = done_v.T.astype(BF16)

        tasks = [
            (side, layer, part * span) for side in range(2) for layer in range(LAYERS) for part in range(layer + 1)
        ]
        pipelined(tasks, score, weigh, gather)
        return 0

    lax.fori_loop(0, PAIRS // 2, attend, 0)
    for load in load_last:
        load.wait()

    def member_rows(other):
        return [
            pl.ds(pl.multiple_of((own ^ turn) * span + (member ^ other) * shard, shard), shard)
            for turn in range(LAYERS)
        ]

    def picked(source, places):
        return jnp.concatenate([source[at, :] for at in places], axis=0)

    stores = []
    for other in range(1, group):
        places = member_rows(other)
        part_v = picked(dv, places)
        down = dot_t(part_v, up_v[...]).astype(BF16)
        stack = jnp.concatenate([picked(dk, places), part_v], axis=1)
        at = pl.ds((other - 1) * WIDTH, WIDTH)
        slope[:, at] = (dot_t(stack, wfc[:, WIDTH : 3 * WIDTH]) + dot(down, low[...])).astype(BF16)
        stores.append(pltpu.make_async_copy(slope.at[:, at], other_h[other - 1], out_sem.at[other]))
        stores[-1].start()
    places = member_rows(0)
    part_v = picked(dv, places)
    down_q = dot_t(dq[...], up_q[...]).astype(BF16)
    down = down_q + dot_t(part_v, up_v[...]).astype(BF16)
    stack = jnp.concatenate([dq[...], picked(dk, places), part_v], axis=1)
    grad_normed = dot_t(stack, wfc[:, : 3 * WIDTH]) + dot(down, low[...])
    for turn in range(LAYERS):
        at = pl.ds(turn * shard, shard)
        standard, scale_inv = norm_parts(rows_of(messages.at[turn], shard))
        part = grad_normed[turn * shard : (turn + 1) * shard]
        gn[at, :] += norm_back(part, standard, scale_inv, gains[0:1, :])
    stores.append(pltpu.make_async_copy(gn, gm_h, out_sem.at[0]))
    stores[-1].start()
    normed_mine = picked(normed, places)
    down_v = dot_t(dv[...], up_v[...]).astype(BF16)
    terms[0] = dot(down_q.T[:16], normed_mine[:, :WIDTH])[:RANK]
    terms[1] = adapter_scale * dot(normed_mine[:, WIDTH:].T[:16], dq[...])[:RANK]
    terms[2] = dot(down_v.T[:16], normed[:, :WIDTH])[LOW_V : LOW_V + RANK]
    terms[3] = adapter_scale * dot(normed[:, WIDTH:].T[:16], dv[...])[LOW_V : LOW_V + RANK]
    for store in stores:
        store.wait()


def closing_kernel(shard, gains, *refs):
    pieces, refs = refs[:LAYERS], refs[LAYERS:]
    gm, outs, refs = refs[0], refs[1 : 1 + NEAR], refs[1 + NEAR :]
    received, grads = refs[:-LAYERS], refs[-LAYERS:]
    for turn in range(LAYERS):
        at = slice(turn * shard, (turn + 1) * shard)
        total = received[0][at, :].astype(F32)
        for other in received[1:]:
            total = total + other[at, :].astype(F32)
        standard, scale_inv = norm_parts(rows_of(pieces[turn], shard))
        grad_rows = gm[at, :] + norm_back(total, standard, scale_inv, gains[0:1, :])
        grads[turn][:shard, :] = grad_rows.astype(BF16)
        if turn < NEAR:
            grads[turn][shard:, :] = outs[turn][...]


def place_kernel(shard, spot, *refs):
    backs, outs, (input_grad, block_output) = far_first(refs[:LAYERS]), refs[LAYERS:-2], refs[-2:]
    for turn in range(LAYERS):
        slot = spot[0] ^ turn
        input_grad[slot] = backs[turn][:shard, :]
        block_output[slot] = backs[turn][shard:, :] if turn < NEAR else outs[turn - NEAR][...]


def cut_rows(whole, slot, message, first, shard):
    for part in range(WIDTH // 128):
        at = slice(first + part * shard, first + (part + 1) * shard)
        message[at, :] = whole[slot, :, part * 128 : (part + 1) * 128]


def pack_kernel(shard, spot, docs, whole, *messages):
    for turn in range(LAYERS):
        slot = spot[0] ^ turn
        cut_rows(whole, slot, messages[turn], 0, shard)
        row = docs[pl.ds(slot, 1), :]
        high = row >> 5
        both = jnp.concatenate([high, row - (high << 5)], axis=0).astype(F32)
        if shard < 128:
            both = jnp.concatenate([both, jnp.zeros((2, 128 - shard), F32)], axis=1)
        both = jnp.concatenate([both, jnp.zeros((14, 128), F32)], axis=0)
        messages[turn][WIDTH // 128 * shard :, :] = both.astype(BF16)


def cut_kernel(shard, spot, pulls, adapters, *refs):
    pieces, (low, up_q, up_v) = refs[:LAYERS], refs[LAYERS:]
    for turn in range(LAYERS):
        cut_rows(pulls, spot[0] ^ turn, pieces[turn], 0, shard)
    none = jnp.zeros((RANK, WIDTH), F32)
    rounded = [adapters[place].astype(BF16).astype(F32) for place in range(4)]
    tail = jnp.zeros((LOW - 2 * LOW_V, WIDTH), F32)
    low[...] = jnp.concatenate([rounded[0], none, rounded[2], none, tail], axis=0).astype(BF16)
    up_q[...] = jnp.concatenate([adapter_scale * rounded[1], none, none, none, tail], axis=0).astype(BF16)
    up_v[...] = jnp.concatenate([none, none, adapter_scale * rounded[3], none, tail], axis=0).astype(BF16)


def adam_update(adapter_grads, adapters, moment_one, moment_two):
    norm_total = jnp.sqrt(jnp.sum(adapter_grads * adapter_grads))
    clipped_grads = adapter_grads * jnp.minimum(1.0, math.sqrt(4.0 * RANK * WIDTH) / norm_total)
    new_moment_one = beta_first * moment_one + (1.0 - beta_first) * clipped_grads
    new_moment_two = beta_second * moment_two + (1.0 - beta_second) * clipped_grads * clipped_grads
    first_hat = new_moment_one / (1.0 - beta_first**step_count)
    second_hat = new_moment_two / (1.0 - beta_second**step_count)
    new_adapters = adapters - learn_rate * (
        first_hat / (jnp.sqrt(second_hat) + adam_floor) + decay_rate * adapters
    )
    return (clipped_grads, new_adapters, new_moment_one, new_moment_two)


VM = pl.BlockSpec(memory_space=pltpu.VMEM)
SM = pl.BlockSpec(memory_space=pltpu.SMEM)
ANY = pl.BlockSpec(memory_space=pl.ANY)


def shaped(dtype, *shape):
    return jax.ShapeDtypeStruct(shape, dtype)


class Routes:
    def __init__(self, slots, blks):
        self.slots, self.blks = slots, blks
        self.group = blks // LAYERS
        self.chips = self.group // 2

    def gathering(self, turn):
        pairs = []
        for slot in range(self.slots):
            for blk in range(self.blks):
                layer, member = blk // self.group, blk % self.group
                target = (2 * (layer ^ turn) + slot % 2) * self.chips + member // 2
                pairs.append((slot * self.blks + blk, (slot - slot % 2 + member % 2) * self.blks + target))
        return pairs

    def returning(self, turn):
        return [(target, source) for source, target in self.gathering(turn)]

    def within(self, other):
        pairs = []
        for slot in range(self.slots):
            for blk in range(self.blks):
                to_slot, to_blk = slot ^ (other & 1), blk ^ (other >> 1)
                pairs.append((slot * self.blks + blk, to_slot * self.blks + to_blk))
        return pairs

    def reaches(self):
        along = [self.blks >> step for step in range(1, self.blks.bit_length())]
        across = [self.blks << step for step in range(self.slots.bit_length() - 1)]
        return across[::-1] + along[2:], [along[1], along[0], along[0] + along[1]]

    def spot(self, slot, blk):
        own = blk // self.chips // 2
        member = (blk % self.chips) * 2 + slot % 2
        return own, member


def body(
    routes,
    activations,
    cotangent,
    norm_gains,
    norm_shifts,
    w_qkv,
    query_value_bias,
    w_out,
    resid_bias,
    w_fc,
    fc_bias,
    w_proj,
    doc_ids,
    adapters,
    moment_one,
    moment_two,
):
    axes = ("slot", "blk")
    group = routes.group
    shard = activations.shape[1]
    span, rows, length = group * shard, LAYERS * shard, LAYERS * group * shard
    width_fc = w_fc.shape[1]
    slot, blk = lax.axis_index("slot"), lax.axis_index("blk")
    home = blk // group
    own, member = routes.spot(slot, blk)
    spot = jnp.stack([home, own, member]).astype(jnp.int32)
    turns = range(LAYERS)

    def pick(whole, turn):
        return lax.dynamic_index_in_dim(whole, home ^ turn, 0, keepdims=False)

    def send(piece, pairs):
        return lax.ppermute(piece, axes, pairs)

    params = pltpu.CompilerParams(vmem_limit_bytes=VMEM_BYTES)
    piece_shape = shaped(BF16, shard, WIDTH)
    part_rows = WIDTH // 128 * shard
    message_rows = part_rows + 16

    messages = pl.pallas_call(
        partial(pack_kernel, shard),
        in_specs=[SM] + [VM] * 2,
        out_specs=[VM] * LAYERS,
        out_shape=[shaped(BF16, message_rows, 128)] * LAYERS,
        name="pack",
    )(spot, doc_ids, activations)
    x_own = [send(messages[turn], routes.gathering(turn)) for turn in turns]
    *cuts, low, up_q, up_v = pl.pallas_call(
        partial(cut_kernel, shard),
        in_specs=[SM, VM, VM],
        out_specs=[VM] * (LAYERS + 3),
        out_shape=[shaped(BF16, part_rows, 128)] * LAYERS + [shaped(BF16, LOW, WIDTH)] * 3,
        name="cut",
    )(spot, cotangent, adapters)
    x_own = [lax.optimization_barrier((piece, low))[0] for piece in x_own]
    pulls = [None] * LAYERS
    for turn in range(NEAR):
        cuts[turn] = lax.optimization_barrier((cuts[turn], x_own[:NEAR]))[0]
        pulls[turn] = send(cuts[turn], routes.gathering(turn))
    for turn in range(NEAR, LAYERS):
        x_own[turn] = lax.optimization_barrier((x_own[turn], pulls[:NEAR]))[0]
        cuts[turn] = lax.optimization_barrier((cuts[turn], x_own[turn]))[0]
        pulls[turn] = send(cuts[turn], routes.gathering(turn))
    pieces = [None] * (LAYERS * group)
    for turn in turns:
        pieces[turn * group] = x_own[turn]
        for other in range(1, group):
            pieces[turn * group + other] = send(x_own[turn], routes.within(other))

    forward = pl.pallas_call(
        partial(forward_kernel, group, shard),
        in_specs=[SM] + [VM] * 8 + [ANY] * (LAYERS * group + 4),
        out_specs=[ANY] * (LAYERS + 7) + [VM] * 2,
        out_shape=[piece_shape] * LAYERS
        + [
            shaped(BF16, length, WIDTH),
            shaped(BF16, length, WIDTH),
            shaped(BF16, WIDTH, 2 * rows),
            shaped(F32, WIDTH, rows),
            shaped(F32, rows, WIDTH),
            shaped(BF16, rows, width_fc),
            shaped(BF16, length, WIDTH + LOW),
            shaped(F32, PAIRS, LAYERS, 2 * shard),
            shaped(jnp.int32, LAYERS, 1, shard),
        ],
        scratch_shapes=[
            pltpu.VMEM((LAYERS * group, message_rows, 128), BF16),
            pltpu.VMEM((length, WIDTH + LOW), BF16),
            pltpu.VMEM((length, WIDTH), BF16),
            pltpu.VMEM((length, WIDTH), BF16),
            pltpu.VMEM((2, VROWS, length), BF16),
            pltpu.VMEM((rows, WIDTH), BF16),
            pltpu.VMEM((WIDTH, 2 * rows), BF16),
            pltpu.VMEM((block_start(LAYERS) * span, 2 * shard), F32),
            pltpu.VMEM((WIDTH, rows), F32),
            pltpu.VMEM((rows, WIDTH), BF16),
            pltpu.VMEM((rows, WIDTH), F32),
            pltpu.VMEM((rows, WIDTH), BF16),
            pltpu.VMEM((rows, WIDTH), F32),
            pltpu.VMEM((rows, width_fc), BF16),
            pltpu.VMEM((rows, WIDTH), BF16),
            pltpu.VMEM((WIDTH + LOW, width_fc), BF16),
            pltpu.VMEM((WIDTH, WIDTH), BF16),
            pltpu.VMEM((width_fc, WIDTH), BF16),
            pltpu.SemaphoreType.DMA((LAYERS * group,)),
            pltpu.SemaphoreType.DMA((6,)),
            pltpu.SemaphoreType.DMA((7 + LAYERS,)),
        ],
        compiler_params=params,
        cost_estimate=pl.CostEstimate(flops=22 * 10**9, bytes_accessed=40 * 2**20, transcendentals=0),
        name="forward",
    )
    results = forward(
        spot,
        norm_gains,
        norm_shifts,
        query_value_bias,
        resid_bias,
        fc_bias.reshape(1, width_fc),
        low,
        up_q,
        up_v,
        *far_first(pieces, group),
        w_qkv,
        w_out,
        w_fc,
        w_proj,
    )
    out_pieces = results[:LAYERS]
    keys, values, spread_q, attended_t, middle, slope, normed, log_total, docs = results[LAYERS:]
    outs = [send(out_pieces[turn], routes.returning(turn)) for turn in range(NEAR, LAYERS)]

    parts = width_fc // 1024
    backward = pl.pallas_call(
        partial(backward_kernel, group, shard),
        in_specs=[SM] + [VM] * 6 + [ANY] * (2 * LAYERS + 11),
        out_specs=[ANY] * group + [VM],
        out_shape=[shaped(F32, rows, WIDTH)]
        + [shaped(BF16, rows, WIDTH)] * (group - 1)
        + [shaped(F32, 4, RANK, WIDTH)],
        scratch_shapes=[
            pltpu.VMEM((rows, WIDTH), BF16),
            pltpu.VMEM((rows, width_fc), BF16),
            pltpu.VMEM((rows, width_fc), BF16),
            pltpu.VMEM((rows, WIDTH), F32),
            pltpu.VMEM((rows, WIDTH), F32),
            pltpu.VMEM((rows, WIDTH), BF16),
            pltpu.VMEM((length, WIDTH), BF16),
            pltpu.VMEM((length, WIDTH), BF16),
            pltpu.VMEM((WIDTH, 2 * rows), BF16),
            pltpu.VMEM((WIDTH, rows), F32),
            pltpu.VMEM((block_start(LAYERS) * span, 2 * shard), F32),
            pltpu.VMEM((2, PAIR, length), BF16),
            pltpu.VMEM((2, PAIR, 2 * rows), BF16),
            pltpu.VMEM((rows, WIDTH), BF16),
            pltpu.VMEM((2, PAIR, 2 * shard), F32),
            pltpu.VMEM((length, WIDTH), BF16),
            pltpu.VMEM((length, WIDTH), BF16),
            pltpu.VMEM((width_fc, WIDTH), BF16),
            pltpu.VMEM((WIDTH, width_fc), BF16),
            pltpu.VMEM((WIDTH, WIDTH), BF16),
            pltpu.VMEM((length, WIDTH + LOW), BF16),
            pltpu.VMEM((LAYERS, WIDTH // 128 * shard, 128), BF16),
            pltpu.SemaphoreType.DMA((LAYERS + 2 * parts + 9,)),
            pltpu.SemaphoreType.DMA((group,)),
        ],
        compiler_params=pltpu.CompilerParams(vmem_limit_bytes=BACK_BYTES),
        cost_estimate=pl.CostEstimate(flops=24 * 10**9, bytes_accessed=40 * 2**20, transcendentals=0),
        name="backward",
    )
    results = backward(
        spot,
        docs,
        norm_gains,
        log_total,
        low,
        up_q,
        up_v,
        *pulls,
        *x_own,
        slope,
        middle,
        spread_q,
        attended_t,
        w_proj,
        w_fc,
        w_out,
        w_qkv,
        keys,
        values,
        normed,
    )
    grad_middle, grad_others, terms = results[0], results[1:-1], results[-1]
    outs, grad_others = lax.optimization_barrier((outs, grad_others))
    received = [send(grad_others[other - 1], routes.within(other)) for other in range(1, group)]

    devices = routes.slots * routes.blks

    def partner(part, reach):
        return send(part, [(device, device ^ reach) for device in range(devices)])

    grad_pieces = pl.pallas_call(
        partial(closing_kernel, shard),
        in_specs=[VM] * (LAYERS + 2 + NEAR + group - 1),
        out_specs=[VM] * LAYERS,
        out_shape=[shaped(BF16, 2 * shard if turn < NEAR else shard, WIDTH) for turn in turns],
        cost_estimate=pl.CostEstimate(flops=10**7, bytes_accessed=6 * 2**20, transcendentals=0),
        name="closing",
    )(norm_gains, *x_own, grad_middle, *out_pieces[:NEAR], *received)
    backs = [None] * LAYERS
    for turn in turns:
        backs[turn] = send(grad_pieces[turn], routes.returning(turn))
    terms = lax.optimization_barrier((terms, backs[0]))[0]
    one_by_one, at_once = routes.reaches()
    for reach in one_by_one:
        terms = terms + partner(terms, reach)
    sums = [terms] + [partner(terms, reach) for reach in at_once]
    while len(sums) > 1:
        sums = [one + two for one, two in zip(sums[::2], sums[1::2])]
    terms = sums[0]
    clipped_grads, new_adapters, new_moment_one, new_moment_two = adam_update(
        terms, adapters, moment_one, moment_two
    )

    input_grad, block_output = pl.pallas_call(
        partial(place_kernel, shard),
        in_specs=[SM] + [VM] * (2 * LAYERS - NEAR),
        out_specs=[VM] * 2,
        out_shape=[shaped(BF16, LAYERS, shard, WIDTH)] * 2,
        cost_estimate=pl.CostEstimate(flops=0, bytes_accessed=4 * 2**20, transcendentals=0),
        name="place",
    )(spot, *far_first(backs), *outs)
    return (block_output, input_grad, clipped_grads, new_adapters, new_moment_one, new_moment_two)


def solution(mesh):
    routes = Routes(mesh.shape["slot"], mesh.shape["blk"])
    rows = P("slot", "blk", None)
    placed = (rows, rows) + (P(),) * 9 + (P("slot", "blk"),) + (P(),) * 3
    return jax.shard_map(
        partial(body, routes),
        mesh=mesh,
        in_specs=placed,
        out_specs=(rows, rows, P(), P(), P(), P()),
        check_vma=False,
    )
```

```python
from functools import partial
import math

import jax
import jax.numpy as jnp
from jax import lax
from jax.experimental import pallas as pl
from jax.experimental.pallas import tpu as pltpu
from jax.sharding import PartitionSpec as P

WIDTH = 1024
HEADS = 16
HEAD_DIM = 64
RANK = 4
LAYERS = 4
PAIRS = HEADS // 2
PAIR = 2 * HEAD_DIM
LOW = 128
LOW_V = 8
FORWARD_PAIRS = 4
BACKWARD_PAIRS = 4
NEAR = 2
VROWS = PAIR + 16

norm_floor = 1e-05
adapter_scale = 8.0
learn_rate = 0.005
beta_first = 0.9
beta_second = 0.999
adam_floor = 1e-08
decay_rate = 0.01
step_count = 100
masked_score = -1e30

F32 = jnp.float32
BF16 = jnp.bfloat16
GELU_C = math.sqrt(2.0 / math.pi)
VMEM_BYTES = 57 * 2**20
BACK_BYTES = 60 * 2**20
SMALL_BYTES = 16 * 2**20


def dot(left, right):
    return jnp.dot(left, right, preferred_element_type=F32)


def dot_t(left, right):
    return lax.dot_general(left, right, (((1,), (1,)), ((), ())), preferred_element_type=F32)


def norm_parts(rows):
    center = rows - jnp.mean(rows, axis=-1, keepdims=True)
    scale_inv = lax.rsqrt(jnp.mean(center * center, axis=-1, keepdims=True) + norm_floor)
    return center * scale_inv, scale_inv


def norm_back(grad_out, standard, scale_inv, gain):
    scaled = grad_out * gain
    return scale_inv * (
        scaled
        - jnp.mean(scaled, axis=-1, keepdims=True)
        - standard * jnp.mean(scaled * standard, axis=-1, keepdims=True)
    )


def gelu_parts(hidden):
    square = hidden * hidden
    bend = jnp.tanh(hidden * (GELU_C + (GELU_C * 0.044715) * square))
    half = 0.5 + 0.5 * bend
    slope = half + hidden * (1.0 - bend * bend) * (0.5 * GELU_C + (1.5 * GELU_C * 0.044715) * square)
    return hidden * half, slope


def block_start(layer):
    return layer * (layer + 1) // 2


def fill_bias(spot, docs, bias, shard, span):
    own, member = spot[1], spot[2]
    for layer in range(LAYERS):
        row = docs[own ^ layer]
        starts = jnp.concatenate([row, row], axis=1)
        keys = span * (layer + 1)
        key_at = lax.broadcasted_iota(jnp.int32, (keys, 2 * shard), 0)
        query_at = lax.broadcasted_iota(jnp.int32, (1, 2 * shard), 1)
        query_at = jnp.where(query_at >= shard, query_at - shard, query_at)
        query_at = query_at + (layer * span + member * shard)
        allowed = (key_at >= starts) & (key_at <= query_at)
        bias[pl.ds(block_start(layer) * span, keys), :] = jnp.where(allowed, 0.0, masked_score)


def spread(block, shard):
    none = jnp.zeros((HEAD_DIM, shard), block.dtype)
    return jnp.concatenate(
        [
            jnp.concatenate([block[:HEAD_DIM], none], axis=1),
            jnp.concatenate([none, block[HEAD_DIM:]], axis=1),
        ],
        axis=0,
    )


def gather_diagonal(block, shard):
    return jnp.concatenate([block[:HEAD_DIM, :shard], block[HEAD_DIM:PAIR, shard:]], axis=0)


def pipelined(tasks, first, second, third):
    ready = first(*tasks[0])
    waiting = None
    for place, task in enumerate(tasks):
        following = first(*tasks[place + 1]) if place + 1 < len(tasks) else None
        weighed = second(*task, *ready)
        if waiting is not None:
            third(*waiting)
        waiting = (*task, *weighed)
        ready = following
    third(*waiting)


def far_first(arrays, each=1):
    return [array for turn in range(LAYERS - 1, -1, -1) for array in arrays[turn * each : (turn + 1) * each]]


def rows_of(message, shard):
    parts = [message[part * shard : (part + 1) * shard, :] for part in range(WIDTH // 128)]
    return jnp.concatenate(parts, axis=1).astype(F32)


def forward_kernel(group, shard, spot, gains, shifts, qv_bias, resid, fc_bias, low, up_q, up_v, *refs):
    pieces, refs = far_first(refs[: LAYERS * group], group), refs[LAYERS * group :]
    wqkv_h, wout_h, wfc_h, wproj_h = refs[:4]
    out_h, refs = refs[4 : 4 + LAYERS], refs[4 + LAYERS :]
    keys_h, values_h, spread_h, attended_h, middle_h, slope_h, normed_h, log_total, docs = refs[:9]
    x, normed, keys, values, values_t, query, spread_q, bias, attended_t, attended = refs[9:19]
    middle, normed_two, total, slope, out, wbuf, wout, wproj = refs[19:27]
    in_sem, w_sem, out_sem, slope_sem = refs[27:]
    span = group * shard
    rows = LAYERS * shard
    width_fc = wfc_h.shape[1]
    own, member = spot[1], spot[2]

    loads = [
        pltpu.make_async_copy(pieces[place].at[pl.ds(0, x.shape[1]), :], x.at[place], in_sem.at[place])
        for place in range(LAYERS * group)
    ]
    for load in loads:
        load.start()
    load_qkv = []
    for place, part in enumerate((1, 2, 0)):
        at = pl.ds(part * WIDTH, WIDTH)
        load_qkv.append(pltpu.make_async_copy(wqkv_h.at[:, at], wbuf.at[pl.ds(0, WIDTH), at], w_sem.at[place]))
    load_qkv[0].start()
    load_out = pltpu.make_async_copy(wout_h, wout, w_sem.at[3])
    load_fc = pltpu.make_async_copy(wfc_h, wbuf.at[pl.ds(0, WIDTH), :], w_sem.at[4])
    load_proj = pltpu.make_async_copy(wproj_h, wproj, w_sem.at[5])
    for turn in range(LAYERS):
        for other in range(group):
            place = turn * group + other
            loads[place].wait()
            if place == LAYERS * group - 1:
                load_qkv[1].start()
                load_qkv[2].start()
            if other == 0:
                numbers = x[place, WIDTH // 128 * shard :, :].astype(F32)
                docs[turn] = (numbers[0:1, :shard] * 32.0 + numbers[1:2, :shard]).astype(jnp.int32)
            standard, _ = norm_parts(rows_of(x.at[place], shard))
            at = pl.ds(pl.multiple_of((own ^ turn) * span + (member ^ other) * shard, shard), shard)
            normed[at, :WIDTH] = (standard * gains[0:1, :] + shifts[0:1, :]).astype(BF16)
    fill_bias(spot, docs, bias, shard, span)
    normed[:, WIDTH:] = dot_t(normed[:, :WIDTH], low[...]).astype(BF16)
    wbuf[WIDTH:, :WIDTH] = up_q[...]
    wbuf[WIDTH:, 2 * WIDTH : 3 * WIDTH] = up_v[...]
    half = WIDTH // 2
    load_qkv[0].wait()
    for first in range(0, WIDTH, half):
        at = pl.ds(first, half)
        keys[:, at] = dot(normed[:, :WIDTH], wbuf[:WIDTH, WIDTH + first : WIDTH + first + half]).astype(BF16)
    load_qkv[1].wait()
    for first in range(0, WIDTH, half):
        at = pl.ds(first, half)
        values[:, at] = (
            dot(normed[...], wbuf[:, 2 * WIDTH + first : 2 * WIDTH + first + half])
            + qv_bias[1:2, at]
        ).astype(BF16)
    own_rows = [pl.ds(pl.multiple_of(layer * span + member * shard, shard), shard) for layer in range(LAYERS)]
    mine = jnp.concatenate([normed[at, :] for at in own_rows], axis=0)
    load_qkv[2].wait()
    query[...] = (
        (dot(mine, wbuf[:, :WIDTH]) + qv_bias[0:1, :]).astype(BF16) * 0.125
    ).astype(BF16)
    load_out.start()
    load_fc.start()
    load_proj.start()
    stores = [
        pltpu.make_async_copy(keys, keys_h, out_sem.at[0]),
        pltpu.make_async_copy(values, values_h, out_sem.at[1]),
        pltpu.make_async_copy(normed, normed_h, out_sem.at[6 + LAYERS]),
    ]
    for store in stores:
        store.start()

    def attend(step, _):
        both = []
        for side in range(FORWARD_PAIRS):
            at = pl.ds(pl.multiple_of((FORWARD_PAIRS * step + side) * PAIR, PAIR), PAIR)
            values_t[side, :PAIR, :] = values[:, at].T
            values_t[side, PAIR:, :] = jnp.ones((VROWS - PAIR, values.shape[0]), BF16)
            for layer in range(LAYERS):
                block = query[layer * shard : (layer + 1) * shard, at].T
                spread_q[at, layer * 2 * shard : (layer + 1) * 2 * shard] = spread(block, shard)
            both.append(at)

        def score(side, layer):
            seen = span * (layer + 1)
            scores = dot(keys[0:seen, both[side]], spread_q[both[side], layer * 2 * shard : (layer + 1) * 2 * shard])
            return (scores + bias[block_start(layer) * span : block_start(layer) * span + seen, :],)

        def weigh(side, layer, scores):
            highest = jnp.max(scores, axis=0, keepdims=True)
            return highest, jnp.exp(scores - highest).astype(BF16)

        def gather(side, layer, highest, weights):
            seen = span * (layer + 1)
            summed = dot(values_t[side, :, 0:seen], weights)
            totals = summed[PAIR : PAIR + 1, :]
            block = gather_diagonal(summed[:PAIR] * (1.0 / totals), shard)
            attended_t[both[side], layer * shard : (layer + 1) * shard] = block
            at = pl.ds(pl.multiple_of((own ^ layer) * shard, shard), shard)
            attended[at, both[side]] = block.T.astype(BF16)
            log_total[FORWARD_PAIRS * step + side, layer : layer + 1, :] = highest + jnp.log(totals)

        tasks = [(side, layer) for side in range(FORWARD_PAIRS) for layer in range(LAYERS)]
        pipelined(tasks, score, weigh, gather)
        return 0

    lax.fori_loop(0, PAIRS // FORWARD_PAIRS, attend, 0)
    stores.append(pltpu.make_async_copy(spread_q, spread_h, out_sem.at[2]))
    stores.append(pltpu.make_async_copy(attended_t, attended_h, out_sem.at[3]))
    for store in stores[3:]:
        store.start()
    load_out.wait()
    branch = dot(attended[...], wout[...]) + resid[0:1, :]
    for turn in range(LAYERS):
        at = pl.ds(turn * shard, shard)
        center = rows_of(x.at[turn * group], shard) + branch[turn * shard : (turn + 1) * shard]
        middle[at, :] = center
        standard, _ = norm_parts(center)
        normed_two[at, :] = (standard * gains[1:2, :] + shifts[1:2, :]).astype(BF16)
    stores.append(pltpu.make_async_copy(middle, middle_h, out_sem.at[4]))
    stores[-1].start()
    load_fc.wait()
    load_proj.wait()
    chunk = 1024
    hidden, acts = {}, {}
    count = width_fc // chunk
    for step in range(count + 2):
        if step < count:
            hidden[step] = dot(normed_two[...], wbuf[:WIDTH, step * chunk : (step + 1) * chunk])
        if 0 <= step - 1 < count:
            at = pl.ds((step - 1) * chunk, chunk)
            act, tilt = gelu_parts(hidden.pop(step - 1) + fc_bias[:, at])
            acts[step - 1] = act.astype(BF16)
            slope[:, at] = tilt.astype(BF16)
            stores.append(pltpu.make_async_copy(slope.at[:, at], slope_h.at[:, at], slope_sem.at[step - 1]))
            stores[-1].start()
        if 0 <= step - 2:
            part = dot(acts.pop(step - 2), wproj[(step - 2) * chunk : (step - 1) * chunk, :])
            if step - 2 == 0:
                total[...] = part
            elif step - 1 < count:
                total[...] += part
            else:
                out[...] = (middle[...] + total[...] + part + resid[1:2, :]).astype(BF16)
    for turn in range(LAYERS):
        stores.append(
            pltpu.make_async_copy(out.at[pl.ds(turn * shard, shard), :], out_h[turn], out_sem.at[6 + turn])
        )
        stores[-1].start()
    for store in stores:
        store.wait()


def backward_kernel(group, shard, spot, docs, gains, log_total, low, up_q, up_v, *refs):
    pulls, refs = refs[:LAYERS], refs[LAYERS:]
    pieces, refs = refs[:LAYERS], refs[LAYERS:]
    slope_h, middle_h, spread_h, attended_h, wproj_h, wfc_h, wout_h, wqkv_h = refs[:8]
    keys_h, values_h, normed_h, refs = refs[8], refs[9], refs[10], refs[11:]
    gm_h, refs = refs[0], refs[1:]
    other_h, terms, refs = refs[: group - 1], refs[group - 1], refs[group:]
    pull, slope, grad_hidden, gn, middle, grad_att, keys, values, spread_q, attended_t = refs[:10]
    bias, keys_t, spread_g, dq, dq_t, dk, dv, wproj, wfc, wout, normed, messages = refs[10:22]
    in_sem, out_sem = refs[22:]
    span = group * shard
    rows = LAYERS * shard
    length = LAYERS * span
    width_fc = wfc_h.shape[1]
    chunk = 1024
    own, member = spot[1], spot[2]

    part_rows = WIDTH // 128 * shard
    load_pull = [
        pltpu.make_async_copy(
            pulls[turn], messages.at[turn], in_sem.at[turn]
        )
        for turn in range(LAYERS)
    ]
    load_proj, load_slope = [], []
    for part in range(width_fc // chunk):
        at = pl.ds(part * chunk, chunk)
        load_proj.append(pltpu.make_async_copy(wproj_h.at[at, :], wproj.at[at, :], in_sem.at[LAYERS + 2 * part]))
        load_slope.append(
            pltpu.make_async_copy(slope_h.at[:, at], slope.at[:, at], in_sem.at[LAYERS + 2 * part + 1])
        )
    base = LAYERS + 2 * (width_fc // chunk)
    load_rest = [
        pltpu.make_async_copy(source, target, in_sem.at[base + place])
        for place, (source, target) in enumerate(
            (
                (wfc_h.at[pl.ds(0, WIDTH // 2), :], wfc.at[pl.ds(0, WIDTH // 2), :]),
                (wfc_h.at[pl.ds(WIDTH // 2, WIDTH // 2), :], wfc.at[pl.ds(WIDTH // 2, WIDTH // 2), :]),
                (middle_h, middle),
                (wout_h, wout),
                (keys_h, keys),
                (values_h, values),
                (spread_h, spread_q),
                (attended_h, attended_t),
                (normed_h, normed),
            )
        )
    ]
    for load in load_pull:
        load.start()
    for part in range(2):
        load_proj[part].start()
        load_slope[part].start()
    for turn in range(LAYERS):
        load_pull[turn].wait()
        pull[turn * shard : (turn + 1) * shard, :] = rows_of(messages.at[turn], shard).astype(BF16)
    for part in range(width_fc // chunk):
        at = pl.ds(part * chunk, chunk)
        load_proj[part].wait()
        load_slope[part].wait()
        if part + 2 < width_fc // chunk:
            load_proj[part + 2].start()
            load_slope[part + 2].start()
        else:
            load_rest[part + 2 - width_fc // chunk].start()
        grad_hidden[:, at] = (dot_t(pull[...], wproj[at, :]) * slope[:, at].astype(F32)).astype(BF16)
    for load in load_rest[2:]:
        load.start()
    fill_bias(spot, docs, bias, shard, span)
    half = WIDTH // 2
    for first in range(0, WIDTH, half):
        at = pl.ds(first, half)
        load_rest[first // half].wait()
        gn[:, at] = dot_t(grad_hidden[...], wfc[at, :])
    load_rest[2].wait()
    load_rest[3].wait()
    standard, scale_inv = norm_parts(middle[...])
    grad_middle = pull[...].astype(F32) + norm_back(gn[...], standard, scale_inv, gains[1:2, :])
    gn[...] = grad_middle
    grad_att[...] = dot_t(grad_middle.astype(BF16), wout[...]).astype(BF16)
    load_last = [pltpu.make_async_copy(wqkv_h, wfc.at[:, pl.ds(0, 3 * WIDTH)], in_sem.at[base + len(load_rest)])]
    load_last.extend(
        pltpu.make_async_copy(pieces[turn].at[pl.ds(0, part_rows), :], messages.at[turn], in_sem.at[turn])
        for turn in range(LAYERS)
    )
    for load in load_last:
        load.start()
    for load in load_rest[4:-1]:
        load.wait()

    def attend(step, _):
        both = [pl.ds(pl.multiple_of((BACKWARD_PAIRS * step + side) * PAIR, PAIR), PAIR) for side in range(BACKWARD_PAIRS)]
        for side in range(BACKWARD_PAIRS):
            keys_t[side] = keys[:, both[side]].T
        deltas = {}
        totals = {}

        def score(side, layer, first):
            cut = pl.ds(layer * 2 * shard, 2 * shard)
            if first == 0:
                at = pl.ds(pl.multiple_of((own ^ layer) * shard, shard), shard)
                block = grad_att[at, both[side]].T
                product = block.astype(F32) * attended_t[both[side], layer * shard : (layer + 1) * shard]
                deltas[side, layer] = jnp.concatenate(
                    [
                        jnp.sum(product[:HEAD_DIM], axis=0, keepdims=True),
                        jnp.sum(product[HEAD_DIM:], axis=0, keepdims=True),
                    ],
                    axis=1,
                )
                spread_g[side, :, layer * 2 * shard : (layer + 1) * 2 * shard] = spread(block, shard)
            key_rows = keys[first : first + span, both[side]]
            value_rows = values[first : first + span, both[side]]
            start = block_start(layer) * span + first
            scores = dot(key_rows, spread_q[both[side], cut]) + bias[start : start + span, :]
            return scores, dot(value_rows, spread_g[side, :, cut])

        def weigh(side, layer, first, scores, grad_chances):
            chances = jnp.exp(scores - log_total[BACKWARD_PAIRS * step + side, layer : layer + 1, :])
            grad_scores = chances * (grad_chances - deltas[side, layer])
            return chances.astype(BF16), grad_scores.astype(BF16)

        def gather(side, layer, first, chances, grad_scores):
            cut = pl.ds(layer * 2 * shard, 2 * shard)
            back_v = dot_t(spread_g[side, :, cut], chances)
            back_k = dot_t(spread_q[both[side], cut], grad_scores)
            back_q = dot(keys_t[side, :, first : first + span], grad_scores)
            part = first // span
            if layer == part:
                totals[side, part] = (back_k, back_v)
            else:
                before = totals[side, part]
                totals[side, part] = (before[0] + back_k, before[1] + back_v)
            if first > 0:
                back_q = back_q + dq_t[side]
            if layer == part:
                at = pl.ds(pl.multiple_of((own ^ layer) * shard, shard), shard)
                dq[at, both[side]] = (gather_diagonal(back_q, shard) * 0.125).T.astype(BF16)
            else:
                dq_t[side] = back_q
            if layer == LAYERS - 1:
                done_k, done_v = totals.pop((side, part))
                dk[first : first + span, both[side]] = done_k.T.astype(BF16)
                dv[first : first + span, both[side]] = done_v.T.astype(BF16)

        tasks = [
            (side, layer, part * span) for side in range(BACKWARD_PAIRS) for layer in range(LAYERS) for part in range(layer + 1)
        ]
        pipelined(tasks, score, weigh, gather)
        return 0

    lax.fori_loop(0, PAIRS // BACKWARD_PAIRS, attend, 0)
    for load in load_last:
        load.wait()

    def member_rows(other):
        return [
            pl.ds(pl.multiple_of((own ^ turn) * span + (member ^ other) * shard, shard), shard)
            for turn in range(LAYERS)
        ]

    def picked(source, places):
        return jnp.concatenate([source[at, :] for at in places], axis=0)

    stores = []
    wfc[:, 3 * WIDTH : 3 * WIDTH + LOW] = low[...].T
    for other in range(1, group):
        places = member_rows(other)
        part_v = picked(dv, places)
        down = dot_t(part_v, up_v[...]).astype(BF16)
        stack = jnp.concatenate([picked(dk, places), part_v, down], axis=1)
        at = pl.ds((other - 1) * WIDTH, WIDTH)
        slope[:, at] = dot_t(stack, wfc[:, WIDTH : 3 * WIDTH + LOW]).astype(BF16)
        stores.append(pltpu.make_async_copy(slope.at[:, at], other_h[other - 1], out_sem.at[other]))
        stores[-1].start()
    places = member_rows(0)
    part_v = picked(dv, places)
    down_q = dot_t(dq[...], up_q[...]).astype(BF16)
    down = down_q + dot_t(part_v, up_v[...]).astype(BF16)
    stack = jnp.concatenate([dq[...], picked(dk, places), part_v, down], axis=1)
    grad_normed = dot_t(stack, wfc[:, : 3 * WIDTH + LOW])
    for turn in range(LAYERS):
        at = pl.ds(turn * shard, shard)
        standard, scale_inv = norm_parts(rows_of(messages.at[turn], shard))
        part = grad_normed[turn * shard : (turn + 1) * shard]
        gn[at, :] += norm_back(part, standard, scale_inv, gains[0:1, :])
    stores.append(pltpu.make_async_copy(gn, gm_h, out_sem.at[0]))
    stores[-1].start()
    load_rest[-1].wait()
    normed_mine = picked(normed, places)
    down_v = dot_t(dv[...], up_v[...]).astype(BF16)
    terms[0] = dot(down_q.T[:16], normed_mine[:, :WIDTH])[:RANK]
    terms[1] = adapter_scale * dot(normed_mine[:, WIDTH:].T[:16], dq[...])[:RANK]
    terms[2] = dot(down_v.T[:16], normed[:, :WIDTH])[LOW_V : LOW_V + RANK]
    terms[3] = adapter_scale * dot(normed[:, WIDTH:].T[:16], dv[...])[LOW_V : LOW_V + RANK]
    for store in stores:
        store.wait()


def closing_kernel(shard, gains, *refs):
    pieces, refs = refs[:LAYERS], refs[LAYERS:]
    gm, outs, refs = refs[0], refs[1 : 1 + NEAR], refs[1 + NEAR :]
    received, grads = refs[:-LAYERS], refs[-LAYERS:]
    for turn in range(LAYERS):
        at = slice(turn * shard, (turn + 1) * shard)
        total = received[0][at, :].astype(F32)
        for other in received[1:]:
            total = total + other[at, :].astype(F32)
        standard, scale_inv = norm_parts(rows_of(pieces[turn], shard))
        grad_rows = gm[at, :] + norm_back(total, standard, scale_inv, gains[0:1, :])
        grads[turn][:shard, :] = grad_rows.astype(BF16)
        if turn < NEAR:
            grads[turn][shard:, :] = outs[turn][...]


def place_kernel(shard, spot, *refs):
    backs, outs, (input_grad, block_output) = far_first(refs[:LAYERS]), refs[LAYERS:-2], refs[-2:]
    for turn in range(LAYERS):
        slot = spot[0] ^ turn
        input_grad[slot] = backs[turn][:shard, :]
        block_output[slot] = backs[turn][shard:, :] if turn < NEAR else outs[turn - NEAR][...]


def cut_rows(whole, slot, message, first, shard):
    for part in range(WIDTH // 128):
        at = slice(first + part * shard, first + (part + 1) * shard)
        message[at, :] = whole[slot, :, part * 128 : (part + 1) * 128]


def pack_kernel(shard, spot, docs, whole, *messages):
    for turn in range(LAYERS):
        slot = spot[0] ^ turn
        cut_rows(whole, slot, messages[turn], 0, shard)
        row = docs[pl.ds(slot, 1), :]
        high = row >> 5
        both = jnp.concatenate([high, row - (high << 5)], axis=0).astype(F32)
        if shard < 128:
            both = jnp.concatenate([both, jnp.zeros((2, 128 - shard), F32)], axis=1)
        both = jnp.concatenate([both, jnp.zeros((14, 128), F32)], axis=0)
        messages[turn][WIDTH // 128 * shard :, :] = both.astype(BF16)


def cut_kernel(shard, spot, pulls, adapters, *refs):
    pieces, (low, up_q, up_v) = refs[:LAYERS], refs[LAYERS:]
    for turn in range(LAYERS):
        cut_rows(pulls, spot[0] ^ turn, pieces[turn], 0, shard)
    none = jnp.zeros((RANK, WIDTH), F32)
    rounded = [adapters[place].astype(BF16).astype(F32) for place in range(4)]
    tail = jnp.zeros((LOW - 2 * LOW_V, WIDTH), F32)
    low[...] = jnp.concatenate([rounded[0], none, rounded[2], none, tail], axis=0).astype(BF16)
    up_q[...] = jnp.concatenate([adapter_scale * rounded[1], none, none, none, tail], axis=0).astype(BF16)
    up_v[...] = jnp.concatenate([none, none, adapter_scale * rounded[3], none, tail], axis=0).astype(BF16)


def adam_update(adapter_grads, adapters, moment_one, moment_two):
    norm_total = jnp.sqrt(jnp.sum(adapter_grads * adapter_grads))
    clipped_grads = adapter_grads * jnp.minimum(1.0, math.sqrt(4.0 * RANK * WIDTH) / norm_total)
    new_moment_one = beta_first * moment_one + (1.0 - beta_first) * clipped_grads
    new_moment_two = beta_second * moment_two + (1.0 - beta_second) * clipped_grads * clipped_grads
    first_hat = new_moment_one / (1.0 - beta_first**step_count)
    second_hat = new_moment_two / (1.0 - beta_second**step_count)
    new_adapters = adapters - learn_rate * (
        first_hat / (jnp.sqrt(second_hat) + adam_floor) + decay_rate * adapters
    )
    return (clipped_grads, new_adapters, new_moment_one, new_moment_two)


VM = pl.BlockSpec(memory_space=pltpu.VMEM)
SM = pl.BlockSpec(memory_space=pltpu.SMEM)
ANY = pl.BlockSpec(memory_space=pl.ANY)


def shaped(dtype, *shape):
    return jax.ShapeDtypeStruct(shape, dtype)


class Routes:
    def __init__(self, slots, blks):
        self.slots, self.blks = slots, blks
        self.group = blks // LAYERS
        self.chips = self.group // 2

    def gathering(self, turn):
        pairs = []
        for slot in range(self.slots):
            for blk in range(self.blks):
                layer, member = blk // self.group, blk % self.group
                target = (2 * (layer ^ turn) + slot % 2) * self.chips + member // 2
                pairs.append((slot * self.blks + blk, (slot - slot % 2 + member % 2) * self.blks + target))
        return pairs

    def returning(self, turn):
        return [(target, source) for source, target in self.gathering(turn)]

    def within(self, other):
        pairs = []
        for slot in range(self.slots):
            for blk in range(self.blks):
                to_slot, to_blk = slot ^ (other & 1), blk ^ (other >> 1)
                pairs.append((slot * self.blks + blk, to_slot * self.blks + to_blk))
        return pairs

    def reaches(self):
        along = [self.blks >> step for step in range(1, self.blks.bit_length())]
        across = [self.blks << step for step in range(self.slots.bit_length() - 1)]
        return across[::-1] + along[2:], [along[1], along[0], along[0] + along[1]]

    def spot(self, slot, blk):
        own = blk // self.chips // 2
        member = (blk % self.chips) * 2 + slot % 2
        return own, member


def body(
    routes,
    activations,
    cotangent,
    norm_gains,
    norm_shifts,
    w_qkv,
    query_value_bias,
    w_out,
    resid_bias,
    w_fc,
    fc_bias,
    w_proj,
    doc_ids,
    adapters,
    moment_one,
    moment_two,
):
    axes = ("slot", "blk")
    group = routes.group
    shard = activations.shape[1]
    span, rows, length = group * shard, LAYERS * shard, LAYERS * group * shard
    width_fc = w_fc.shape[1]
    slot, blk = lax.axis_index("slot"), lax.axis_index("blk")
    home = blk // group
    own, member = routes.spot(slot, blk)
    spot = jnp.stack([home, own, member]).astype(jnp.int32)
    turns = range(LAYERS)

    def pick(whole, turn):
        return lax.dynamic_index_in_dim(whole, home ^ turn, 0, keepdims=False)

    def send(piece, pairs):
        return lax.ppermute(piece, axes, pairs)

    params = pltpu.CompilerParams(vmem_limit_bytes=VMEM_BYTES)
    piece_shape = shaped(BF16, shard, WIDTH)
    part_rows = WIDTH // 128 * shard
    message_rows = part_rows + 16

    messages = pl.pallas_call(
        partial(pack_kernel, shard),
        in_specs=[SM] + [VM] * 2,
        out_specs=[VM] * LAYERS,
        out_shape=[shaped(BF16, message_rows, 128)] * LAYERS,
        name="pack",
    )(spot, doc_ids, activations)
    x_own = [send(messages[turn], routes.gathering(turn)) for turn in turns]
    *cuts, low, up_q, up_v = pl.pallas_call(
        partial(cut_kernel, shard),
        in_specs=[SM, VM, VM],
        out_specs=[VM] * (LAYERS + 3),
        out_shape=[shaped(BF16, part_rows, 128)] * LAYERS + [shaped(BF16, LOW, WIDTH)] * 3,
        name="cut",
    )(spot, cotangent, adapters)
    x_own = [lax.optimization_barrier((piece, low))[0] for piece in x_own]
    pulls = [None] * LAYERS
    for turn in range(NEAR):
        cuts[turn] = lax.optimization_barrier((cuts[turn], x_own[:NEAR]))[0]
        pulls[turn] = send(cuts[turn], routes.gathering(turn))
    for turn in range(NEAR, LAYERS):
        x_own[turn] = lax.optimization_barrier((x_own[turn], pulls[:NEAR]))[0]
        cuts[turn] = lax.optimization_barrier((cuts[turn], x_own[turn]))[0]
        pulls[turn] = send(cuts[turn], routes.gathering(turn))
    pieces = [None] * (LAYERS * group)
    for turn in turns:
        pieces[turn * group] = x_own[turn]
        for other in range(1, group):
            pieces[turn * group + other] = send(x_own[turn], routes.within(other))

    forward = pl.pallas_call(
        partial(forward_kernel, group, shard),
        in_specs=[SM] + [VM] * 8 + [ANY] * (LAYERS * group + 4),
        out_specs=[ANY] * (LAYERS + 7) + [VM] * 2,
        out_shape=[piece_shape] * LAYERS
        + [
            shaped(BF16, length, WIDTH),
            shaped(BF16, length, WIDTH),
            shaped(BF16, WIDTH, 2 * rows),
            shaped(F32, WIDTH, rows),
            shaped(F32, rows, WIDTH),
            shaped(BF16, rows, width_fc),
            shaped(BF16, length, WIDTH + LOW),
            shaped(F32, PAIRS, LAYERS, 2 * shard),
            shaped(jnp.int32, LAYERS, 1, shard),
        ],
        scratch_shapes=[
            pltpu.VMEM((LAYERS * group, message_rows, 128), BF16),
            pltpu.VMEM((length, WIDTH + LOW), BF16),
            pltpu.VMEM((length, WIDTH), BF16),
            pltpu.VMEM((length, WIDTH), BF16),
            pltpu.VMEM((FORWARD_PAIRS, VROWS, length), BF16),
            pltpu.VMEM((rows, WIDTH), BF16),
            pltpu.VMEM((WIDTH, 2 * rows), BF16),
            pltpu.VMEM((block_start(LAYERS) * span, 2 * shard), F32),
            pltpu.VMEM((WIDTH, rows), F32),
            pltpu.VMEM((rows, WIDTH), BF16),
            pltpu.VMEM((rows, WIDTH), F32),
            pltpu.VMEM((rows, WIDTH), BF16),
            pltpu.VMEM((rows, WIDTH), F32),
            pltpu.VMEM((rows, width_fc), BF16),
            pltpu.VMEM((rows, WIDTH), BF16),
            pltpu.VMEM((WIDTH + LOW, width_fc), BF16),
            pltpu.VMEM((WIDTH, WIDTH), BF16),
            pltpu.VMEM((width_fc, WIDTH), BF16),
            pltpu.SemaphoreType.DMA((LAYERS * group,)),
            pltpu.SemaphoreType.DMA((6,)),
            pltpu.SemaphoreType.DMA((7 + LAYERS,)),
            pltpu.SemaphoreType.DMA((width_fc // 1024,)),
        ],
        compiler_params=params,
        cost_estimate=pl.CostEstimate(flops=22 * 10**9, bytes_accessed=40 * 2**20, transcendentals=0),
        name="forward",
    )
    results = forward(
        spot,
        norm_gains,
        norm_shifts,
        query_value_bias,
        resid_bias,
        fc_bias.reshape(1, width_fc),
        low,
        up_q,
        up_v,
        *far_first(pieces, group),
        w_qkv,
        w_out,
        w_fc,
        w_proj,
    )
    out_pieces = results[:LAYERS]
    keys, values, spread_q, attended_t, middle, slope, normed, log_total, docs = results[LAYERS:]
    outs = [send(out_pieces[turn], routes.returning(turn)) for turn in range(NEAR, LAYERS)]

    parts = width_fc // 1024
    backward = pl.pallas_call(
        partial(backward_kernel, group, shard),
        in_specs=[SM] + [VM] * 6 + [ANY] * (2 * LAYERS + 11),
        out_specs=[ANY] * group + [VM],
        out_shape=[shaped(F32, rows, WIDTH)]
        + [shaped(BF16, rows, WIDTH)] * (group - 1)
        + [shaped(F32, 4, RANK, WIDTH)],
        scratch_shapes=[
            pltpu.VMEM((rows, WIDTH), BF16),
            pltpu.VMEM((rows, width_fc), BF16),
            pltpu.VMEM((rows, width_fc), BF16),
            pltpu.VMEM((rows, WIDTH), F32),
            pltpu.VMEM((rows, WIDTH), F32),
            pltpu.VMEM((rows, WIDTH), BF16),
            pltpu.VMEM((length, WIDTH), BF16),
            pltpu.VMEM((length, WIDTH), BF16),
            pltpu.VMEM((WIDTH, 2 * rows), BF16),
            pltpu.VMEM((WIDTH, rows), F32),
            pltpu.VMEM((block_start(LAYERS) * span, 2 * shard), F32),
            pltpu.VMEM((BACKWARD_PAIRS, PAIR, length), BF16),
            pltpu.VMEM((BACKWARD_PAIRS, PAIR, 2 * rows), BF16),
            pltpu.VMEM((rows, WIDTH), BF16),
            pltpu.VMEM((BACKWARD_PAIRS, PAIR, 2 * shard), F32),
            pltpu.VMEM((length, WIDTH), BF16),
            pltpu.VMEM((length, WIDTH), BF16),
            pltpu.VMEM((width_fc, WIDTH), BF16),
            pltpu.VMEM((WIDTH, width_fc), BF16),
            pltpu.VMEM((WIDTH, WIDTH), BF16),
            pltpu.VMEM((length, WIDTH + LOW), BF16),
            pltpu.VMEM((LAYERS, WIDTH // 128 * shard, 128), BF16),
            pltpu.SemaphoreType.DMA((LAYERS + 2 * parts + 10,)),
            pltpu.SemaphoreType.DMA((group,)),
        ],
        compiler_params=pltpu.CompilerParams(vmem_limit_bytes=BACK_BYTES),
        cost_estimate=pl.CostEstimate(flops=24 * 10**9, bytes_accessed=40 * 2**20, transcendentals=0),
        name="backward",
    )
    results = backward(
        spot,
        docs,
        norm_gains,
        log_total,
        low,
        up_q,
        up_v,
        *pulls,
        *x_own,
        slope,
        middle,
        spread_q,
        attended_t,
        w_proj,
        w_fc,
        w_out,
        w_qkv,
        keys,
        values,
        normed,
    )
    grad_middle, grad_others, terms = results[0], results[1:-1], results[-1]
    outs, grad_others = lax.optimization_barrier((outs, grad_others))
    received = [send(grad_others[other - 1], routes.within(other)) for other in range(1, group)]

    devices = routes.slots * routes.blks

    def partner(part, reach):
        return send(part, [(device, device ^ reach) for device in range(devices)])

    grad_pieces = pl.pallas_call(
        partial(closing_kernel, shard),
        in_specs=[VM] * (LAYERS + 2 + NEAR + group - 1),
        out_specs=[VM] * LAYERS,
        out_shape=[shaped(BF16, 2 * shard if turn < NEAR else shard, WIDTH) for turn in turns],
        compiler_params=pltpu.CompilerParams(vmem_limit_bytes=SMALL_BYTES),
        cost_estimate=pl.CostEstimate(flops=10**7, bytes_accessed=6 * 2**20, transcendentals=0),
        name="closing",
    )(norm_gains, *x_own, grad_middle, *out_pieces[:NEAR], *received)
    backs = [None] * LAYERS
    for turn in turns:
        backs[turn] = send(grad_pieces[turn], routes.returning(turn))
    one_by_one, at_once = routes.reaches()
    terms = lax.optimization_barrier((terms, grad_pieces[0]))[0]
    for place, reach in enumerate(one_by_one):
        if place == len(one_by_one) - 1:
            terms = lax.optimization_barrier((terms, backs[0]))[0]
        terms = terms + partner(terms, reach)
    sums = [terms] + [partner(terms, reach) for reach in at_once]
    while len(sums) > 1:
        sums = [one + two for one, two in zip(sums[::2], sums[1::2])]
    terms = sums[0]
    clipped_grads, new_adapters, new_moment_one, new_moment_two = adam_update(
        terms, adapters, moment_one, moment_two
    )

    input_grad, block_output = pl.pallas_call(
        partial(place_kernel, shard),
        in_specs=[SM] + [VM] * (2 * LAYERS - NEAR),
        out_specs=[VM] * 2,
        out_shape=[shaped(BF16, LAYERS, shard, WIDTH)] * 2,
        compiler_params=pltpu.CompilerParams(vmem_limit_bytes=SMALL_BYTES),
        cost_estimate=pl.CostEstimate(flops=0, bytes_accessed=4 * 2**20, transcendentals=0),
        name="place",
    )(spot, *far_first(backs), *outs)
    return (block_output, input_grad, clipped_grads, new_adapters, new_moment_one, new_moment_two)


def solution(mesh):
    routes = Routes(mesh.shape["slot"], mesh.shape["blk"])
    rows = P("slot", "blk", None)
    placed = (rows, rows) + (P(),) * 9 + (P("slot", "blk"),) + (P(),) * 3
    return jax.shard_map(
        partial(body, routes),
        mesh=mesh,
        in_specs=placed,
        out_specs=(rows, rows, P(), P(), P(), P()),
        check_vma=False,
    )
```

```python
from functools import partial
import math

import jax
import jax.numpy as jnp
from jax import lax
from jax.experimental import pallas as pl
from jax.experimental.pallas import tpu as pltpu
from jax.sharding import PartitionSpec as P

WIDTH = 1024
HEADS = 16
HEAD_DIM = 64
RANK = 4
LAYERS = 4
PAIRS = HEADS // 2
PAIR = 2 * HEAD_DIM
LOW = 128
LOW_V = 8
FORWARD_PAIRS = 4
BACKWARD_PAIRS = 4
NEAR = 2
VROWS = PAIR + 16

norm_floor = 1e-05
adapter_scale = 8.0
learn_rate = 0.005
beta_first = 0.9
beta_second = 0.999
adam_floor = 1e-08
decay_rate = 0.01
step_count = 100
masked_score = -1e30

F32 = jnp.float32
BF16 = jnp.bfloat16
GELU_C = math.sqrt(2.0 / math.pi)
VMEM_BYTES = 57 * 2**20
BACK_BYTES = 60 * 2**20
SMALL_BYTES = 16 * 2**20


def dot(left, right):
    return jnp.dot(left, right, preferred_element_type=F32)


def dot_t(left, right):
    return lax.dot_general(left, right, (((1,), (1,)), ((), ())), preferred_element_type=F32)


def norm_parts(rows):
    center = rows - jnp.mean(rows, axis=-1, keepdims=True)
    scale_inv = lax.rsqrt(jnp.mean(center * center, axis=-1, keepdims=True) + norm_floor)
    return center * scale_inv, scale_inv


def norm_back(grad_out, standard, scale_inv, gain):
    scaled = grad_out * gain
    return scale_inv * (
        scaled
        - jnp.mean(scaled, axis=-1, keepdims=True)
        - standard * jnp.mean(scaled * standard, axis=-1, keepdims=True)
    )


def gelu_parts(hidden):
    square = hidden * hidden
    bend = jnp.tanh(hidden * (GELU_C + (GELU_C * 0.044715) * square))
    half = 0.5 + 0.5 * bend
    slope = half + hidden * (1.0 - bend * bend) * (0.5 * GELU_C + (1.5 * GELU_C * 0.044715) * square)
    return hidden * half, slope


def block_start(layer):
    return layer * (layer + 1) // 2


def fill_bias(spot, docs, bias, shard, span):
    own, member = spot[1], spot[2]
    for layer in range(LAYERS):
        row = docs[own ^ layer]
        starts = jnp.concatenate([row, row], axis=1)
        keys = span * (layer + 1)
        key_at = lax.broadcasted_iota(jnp.int32, (keys, 2 * shard), 0)
        query_at = lax.broadcasted_iota(jnp.int32, (1, 2 * shard), 1)
        query_at = jnp.where(query_at >= shard, query_at - shard, query_at)
        query_at = query_at + (layer * span + member * shard)
        allowed = (key_at >= starts) & (key_at <= query_at)
        bias[pl.ds(block_start(layer) * span, keys), :] = jnp.where(allowed, 0.0, masked_score)


def spread(block, shard):
    none = jnp.zeros((HEAD_DIM, shard), block.dtype)
    return jnp.concatenate(
        [
            jnp.concatenate([block[:HEAD_DIM], none], axis=1),
            jnp.concatenate([none, block[HEAD_DIM:]], axis=1),
        ],
        axis=0,
    )


def gather_diagonal(block, shard):
    return jnp.concatenate([block[:HEAD_DIM, :shard], block[HEAD_DIM:PAIR, shard:]], axis=0)


def pipelined(tasks, first, second, third):
    ready = first(*tasks[0])
    waiting = None
    for place, task in enumerate(tasks):
        following = first(*tasks[place + 1]) if place + 1 < len(tasks) else None
        weighed = second(*task, *ready)
        if waiting is not None:
            third(*waiting)
        waiting = (*task, *weighed)
        ready = following
    third(*waiting)


def far_first(arrays, each=1):
    return [array for turn in range(LAYERS - 1, -1, -1) for array in arrays[turn * each : (turn + 1) * each]]


def rows_of(message, shard):
    parts = [message[part * shard : (part + 1) * shard, :] for part in range(WIDTH // 128)]
    return jnp.concatenate(parts, axis=1).astype(F32)


def forward_kernel(group, shard, spot, gains, shifts, qv_bias, resid, fc_bias, low, up_q, up_v, *refs):
    pieces, refs = far_first(refs[: LAYERS * group], group), refs[LAYERS * group :]
    wqkv_h, wout_h, wfc_h, wproj_h = refs[:4]
    out_h, refs = refs[4 : 4 + LAYERS], refs[4 + LAYERS :]
    keys_h, values_h, spread_h, attended_h, middle_h, slope_h, normed_h, log_total, docs = refs[:9]
    x, normed, keys, values, values_t, query, spread_q, bias, attended_t, attended = refs[9:19]
    middle, normed_two, total, slope, out, wbuf, wout, wproj = refs[19:27]
    in_sem, w_sem, out_sem, slope_sem = refs[27:]
    span = group * shard
    rows = LAYERS * shard
    width_fc = wfc_h.shape[1]
    own, member = spot[1], spot[2]

    loads = [
        pltpu.make_async_copy(pieces[place].at[pl.ds(0, x.shape[1]), :], x.at[place], in_sem.at[place])
        for place in range(LAYERS * group)
    ]
    for load in loads:
        load.start()
    load_qkv = []
    for place, part in enumerate((1, 2, 0)):
        at = pl.ds(part * WIDTH, WIDTH)
        load_qkv.append(pltpu.make_async_copy(wqkv_h.at[:, at], wbuf.at[pl.ds(0, WIDTH), at], w_sem.at[place]))
    load_qkv[0].start()
    load_out = pltpu.make_async_copy(wout_h, wout, w_sem.at[3])
    load_fc = pltpu.make_async_copy(wfc_h, wbuf.at[pl.ds(0, WIDTH), :], w_sem.at[4])
    load_proj = pltpu.make_async_copy(wproj_h, wproj, w_sem.at[5])
    for turn in range(LAYERS):
        for other in range(group):
            place = turn * group + other
            loads[place].wait()
            if place == LAYERS * group - 1:
                load_qkv[1].start()
                load_qkv[2].start()
            if other == 0:
                numbers = x[place, WIDTH // 128 * shard :, :].astype(F32)
                docs[turn] = (numbers[0:1, :shard] * 32.0 + numbers[1:2, :shard]).astype(jnp.int32)
            standard, _ = norm_parts(rows_of(x.at[place], shard))
            at = pl.ds(pl.multiple_of((own ^ turn) * span + (member ^ other) * shard, shard), shard)
            normed[at, :WIDTH] = (standard * gains[0:1, :] + shifts[0:1, :]).astype(BF16)
    fill_bias(spot, docs, bias, shard, span)
    normed[:, WIDTH:] = dot_t(normed[:, :WIDTH], low[...]).astype(BF16)
    wbuf[WIDTH:, :WIDTH] = up_q[...]
    wbuf[WIDTH:, 2 * WIDTH : 3 * WIDTH] = up_v[...]
    half = WIDTH // 2
    load_qkv[0].wait()
    for first in range(0, WIDTH, half):
        at = pl.ds(first, half)
        keys[:, at] = dot(normed[:, :WIDTH], wbuf[:WIDTH, WIDTH + first : WIDTH + first + half]).astype(BF16)
    load_qkv[1].wait()
    for first in range(0, WIDTH, half):
        at = pl.ds(first, half)
        values[:, at] = (
            dot(normed[...], wbuf[:, 2 * WIDTH + first : 2 * WIDTH + first + half])
            + qv_bias[1:2, at]
        ).astype(BF16)
    own_rows = [pl.ds(pl.multiple_of(layer * span + member * shard, shard), shard) for layer in range(LAYERS)]
    mine = jnp.concatenate([normed[at, :] for at in own_rows], axis=0)
    load_qkv[2].wait()
    query[...] = (
        (dot(mine, wbuf[:, :WIDTH]) + qv_bias[0:1, :]).astype(BF16) * 0.125
    ).astype(BF16)
    load_out.start()
    load_fc.start()
    load_proj.start()
    stores = [
        pltpu.make_async_copy(keys, keys_h, out_sem.at[0]),
        pltpu.make_async_copy(values, values_h, out_sem.at[1]),
        pltpu.make_async_copy(normed, normed_h, out_sem.at[6 + LAYERS]),
    ]
    for store in stores:
        store.start()

    def attend(step, _):
        both = []
        for side in range(FORWARD_PAIRS):
            at = pl.ds(pl.multiple_of((FORWARD_PAIRS * step + side) * PAIR, PAIR), PAIR)
            values_t[side, :PAIR, :] = values[:, at].T
            values_t[side, PAIR:, :] = jnp.ones((VROWS - PAIR, values.shape[0]), BF16)
            for layer in range(LAYERS):
                block = query[layer * shard : (layer + 1) * shard, at].T
                spread_q[at, layer * 2 * shard : (layer + 1) * 2 * shard] = spread(block, shard)
            both.append(at)

        def score(side, layer):
            seen = span * (layer + 1)
            scores = dot(keys[0:seen, both[side]], spread_q[both[side], layer * 2 * shard : (layer + 1) * 2 * shard])
            return (scores + bias[block_start(layer) * span : block_start(layer) * span + seen, :],)

        def weigh(side, layer, scores):
            highest = jnp.max(scores, axis=0, keepdims=True)
            return highest, jnp.exp(scores - highest).astype(BF16)

        def gather(side, layer, highest, weights):
            seen = span * (layer + 1)
            summed = dot(values_t[side, :, 0:seen], weights)
            totals = summed[PAIR : PAIR + 1, :]
            block = gather_diagonal(summed[:PAIR] * (1.0 / totals), shard)
            attended_t[both[side], layer * shard : (layer + 1) * shard] = block
            at = pl.ds(pl.multiple_of((own ^ layer) * shard, shard), shard)
            attended[at, both[side]] = block.T.astype(BF16)
            log_total[FORWARD_PAIRS * step + side, layer : layer + 1, :] = highest + jnp.log(totals)

        tasks = [(side, layer) for side in range(FORWARD_PAIRS) for layer in range(LAYERS)]
        pipelined(tasks, score, weigh, gather)
        return 0

    lax.fori_loop(0, PAIRS // FORWARD_PAIRS, attend, 0)
    stores.append(pltpu.make_async_copy(spread_q, spread_h, out_sem.at[2]))
    stores.append(pltpu.make_async_copy(attended_t, attended_h, out_sem.at[3]))
    for store in stores[3:]:
        store.start()
    load_out.wait()
    branch = dot(attended[...], wout[...]) + resid[0:1, :]
    for turn in range(LAYERS):
        at = pl.ds(turn * shard, shard)
        center = rows_of(x.at[turn * group], shard) + branch[turn * shard : (turn + 1) * shard]
        middle[at, :] = center
        standard, _ = norm_parts(center)
        normed_two[at, :] = (standard * gains[1:2, :] + shifts[1:2, :]).astype(BF16)
    stores.append(pltpu.make_async_copy(middle, middle_h, out_sem.at[4]))
    stores[-1].start()
    load_fc.wait()
    load_proj.wait()
    chunk = 1024
    hidden, acts = {}, {}
    count = width_fc // chunk
    for step in range(count + 2):
        if step < count:
            hidden[step] = dot(normed_two[...], wbuf[:WIDTH, step * chunk : (step + 1) * chunk])
        if 0 <= step - 1 < count:
            at = pl.ds((step - 1) * chunk, chunk)
            act, tilt = gelu_parts(hidden.pop(step - 1) + fc_bias[:, at])
            acts[step - 1] = act.astype(BF16)
            slope[:, at] = tilt.astype(BF16)
            stores.append(pltpu.make_async_copy(slope.at[:, at], slope_h.at[:, at], slope_sem.at[step - 1]))
            stores[-1].start()
        if 0 <= step - 2:
            part = dot(acts.pop(step - 2), wproj[(step - 2) * chunk : (step - 1) * chunk, :])
            if step - 2 == 0:
                total[...] = part
            elif step - 1 < count:
                total[...] += part
            else:
                out[...] = (middle[...] + total[...] + part + resid[1:2, :]).astype(BF16)
    for turn in range(LAYERS):
        stores.append(
            pltpu.make_async_copy(out.at[pl.ds(turn * shard, shard), :], out_h[turn], out_sem.at[6 + turn])
        )
        stores[-1].start()
    for store in stores:
        store.wait()


def backward_kernel(group, shard, spot, docs, gains, log_total, low, up_q, up_v, *refs):
    pulls, refs = refs[:LAYERS], refs[LAYERS:]
    pieces, refs = refs[:LAYERS], refs[LAYERS:]
    slope_h, middle_h, spread_h, attended_h, wproj_h, wfc_h, wout_h, wqkv_h = refs[:8]
    keys_h, values_h, normed_h, refs = refs[8], refs[9], refs[10], refs[11:]
    gm_h, refs = refs[0], refs[1:]
    other_h, terms, refs = refs[: group - 1], refs[group - 1], refs[group:]
    pull, slope, grad_hidden, gn, middle, grad_att, keys, values, spread_q, attended_t = refs[:10]
    bias, keys_t, spread_g, dq, dq_t, dk, dv, wproj, wfc, wout, normed, messages = refs[10:22]
    in_sem, out_sem = refs[22:]
    span = group * shard
    rows = LAYERS * shard
    length = LAYERS * span
    width_fc = wfc_h.shape[1]
    chunk = 1024
    own, member = spot[1], spot[2]

    part_rows = WIDTH // 128 * shard
    load_pull = [
        pltpu.make_async_copy(
            pulls[turn], messages.at[turn], in_sem.at[turn]
        )
        for turn in range(LAYERS)
    ]
    load_proj, load_slope = [], []
    for part in range(width_fc // chunk):
        at = pl.ds(part * chunk, chunk)
        load_proj.append(pltpu.make_async_copy(wproj_h.at[at, :], wproj.at[at, :], in_sem.at[LAYERS + 2 * part]))
        load_slope.append(
            pltpu.make_async_copy(slope_h.at[:, at], slope.at[:, at], in_sem.at[LAYERS + 2 * part + 1])
        )
    base = LAYERS + 2 * (width_fc // chunk)
    load_rest = [
        pltpu.make_async_copy(source, target, in_sem.at[base + place])
        for place, (source, target) in enumerate(
            (
                (wfc_h.at[pl.ds(0, WIDTH // 2), :], wfc.at[pl.ds(0, WIDTH // 2), :]),
                (wfc_h.at[pl.ds(WIDTH // 2, WIDTH // 2), :], wfc.at[pl.ds(WIDTH // 2, WIDTH // 2), :]),
                (middle_h, middle),
                (wout_h, wout),
                (keys_h, keys),
                (values_h, values),
                (spread_h, spread_q),
                (attended_h, attended_t),
                (normed_h, normed),
            )
        )
    ]
    for load in load_pull:
        load.start()
    for part in range(2):
        load_proj[part].start()
        load_slope[part].start()
    for turn in range(LAYERS):
        load_pull[turn].wait()
        pull[turn * shard : (turn + 1) * shard, :] = rows_of(messages.at[turn], shard).astype(BF16)
    for part in range(width_fc // chunk):
        at = pl.ds(part * chunk, chunk)
        load_proj[part].wait()
        load_slope[part].wait()
        if part + 2 < width_fc // chunk:
            load_proj[part + 2].start()
            load_slope[part + 2].start()
        else:
            load_rest[part + 2 - width_fc // chunk].start()
        grad_hidden[:, at] = (dot_t(pull[...], wproj[at, :]) * slope[:, at].astype(F32)).astype(BF16)
    for load in load_rest[2:]:
        load.start()
    fill_bias(spot, docs, bias, shard, span)
    half = WIDTH // 2
    for first in range(0, WIDTH, half):
        at = pl.ds(first, half)
        load_rest[first // half].wait()
        gn[:, at] = dot_t(grad_hidden[...], wfc[at, :])
    load_rest[2].wait()
    load_rest[3].wait()
    standard, scale_inv = norm_parts(middle[...])
    grad_middle = pull[...].astype(F32) + norm_back(gn[...], standard, scale_inv, gains[1:2, :])
    gn[...] = grad_middle
    grad_att[...] = dot_t(grad_middle.astype(BF16), wout[...]).astype(BF16)
    load_last = [pltpu.make_async_copy(wqkv_h, wfc.at[:, pl.ds(0, 3 * WIDTH)], in_sem.at[base + len(load_rest)])]
    load_last.extend(
        pltpu.make_async_copy(pieces[turn].at[pl.ds(0, part_rows), :], messages.at[turn], in_sem.at[turn])
        for turn in range(LAYERS)
    )
    for load in load_last:
        load.start()
    for load in load_rest[4:-1]:
        load.wait()

    def attend(step, _):
        both = [pl.ds(pl.multiple_of((BACKWARD_PAIRS * step + side) * PAIR, PAIR), PAIR) for side in range(BACKWARD_PAIRS)]
        for side in range(BACKWARD_PAIRS):
            keys_t[side] = keys[:, both[side]].T
        deltas = {}
        totals = {}

        def score(side, layer, first):
            cut = pl.ds(layer * 2 * shard, 2 * shard)
            if first == 0:
                at = pl.ds(pl.multiple_of((own ^ layer) * shard, shard), shard)
                block = grad_att[at, both[side]].T
                product = block.astype(F32) * attended_t[both[side], layer * shard : (layer + 1) * shard]
                deltas[side, layer] = jnp.concatenate(
                    [
                        jnp.sum(product[:HEAD_DIM], axis=0, keepdims=True),
                        jnp.sum(product[HEAD_DIM:], axis=0, keepdims=True),
                    ],
                    axis=1,
                )
                spread_g[side, :, layer * 2 * shard : (layer + 1) * 2 * shard] = spread(block, shard)
            key_rows = keys[first : first + span, both[side]]
            value_rows = values[first : first + span, both[side]]
            start = block_start(layer) * span + first
            scores = dot(key_rows, spread_q[both[side], cut]) + bias[start : start + span, :]
            return scores, dot(value_rows, spread_g[side, :, cut])

        def weigh(side, layer, first, scores, grad_chances):
            chances = jnp.exp(scores - log_total[BACKWARD_PAIRS * step + side, layer : layer + 1, :])
            grad_scores = chances * (grad_chances - deltas[side, layer])
            return chances.astype(BF16), grad_scores.astype(BF16)

        def gather(side, layer, first, chances, grad_scores):
            cut = pl.ds(layer * 2 * shard, 2 * shard)
            back_v = dot_t(spread_g[side, :, cut], chances)
            back_k = dot_t(spread_q[both[side], cut], grad_scores)
            back_q = dot(keys_t[side, :, first : first + span], grad_scores)
            part = first // span
            if layer == part:
                totals[side, part] = (back_k, back_v)
            else:
                before = totals[side, part]
                totals[side, part] = (before[0] + back_k, before[1] + back_v)
            if first > 0:
                back_q = back_q + dq_t[side]
            if layer == part:
                at = pl.ds(pl.multiple_of((own ^ layer) * shard, shard), shard)
                dq[at, both[side]] = (gather_diagonal(back_q, shard) * 0.125).T.astype(BF16)
            else:
                dq_t[side] = back_q
            if layer == LAYERS - 1:
                done_k, done_v = totals.pop((side, part))
                dk[first : first + span, both[side]] = done_k.T.astype(BF16)
                dv[first : first + span, both[side]] = done_v.T.astype(BF16)

        tasks = [
            (side, layer, part * span) for side in range(BACKWARD_PAIRS) for layer in range(LAYERS) for part in range(layer + 1)
        ]
        pipelined(tasks, score, weigh, gather)
        return 0

    lax.fori_loop(0, PAIRS // BACKWARD_PAIRS, attend, 0)
    for load in load_last:
        load.wait()

    def member_rows(other):
        return [
            pl.ds(pl.multiple_of((own ^ turn) * span + (member ^ other) * shard, shard), shard)
            for turn in range(LAYERS)
        ]

    def picked(source, places):
        return jnp.concatenate([source[at, :] for at in places], axis=0)

    stores = []
    wfc[:, 3 * WIDTH : 3 * WIDTH + LOW] = low[...].T
    for other in range(1, group):
        places = member_rows(other)
        part_v = picked(dv, places)
        down = dot_t(part_v, up_v[...]).astype(BF16)
        stack = jnp.concatenate([picked(dk, places), part_v, down], axis=1)
        at = pl.ds((other - 1) * WIDTH, WIDTH)
        slope[:, at] = dot_t(stack, wfc[:, WIDTH : 3 * WIDTH + LOW]).astype(BF16)
        stores.append(pltpu.make_async_copy(slope.at[:, at], other_h[other - 1], out_sem.at[other]))
        stores[-1].start()
    places = member_rows(0)
    part_v = picked(dv, places)
    down_q = dot_t(dq[...], up_q[...]).astype(BF16)
    down = down_q + dot_t(part_v, up_v[...]).astype(BF16)
    stack = jnp.concatenate([dq[...], picked(dk, places), part_v, down], axis=1)
    grad_normed = dot_t(stack, wfc[:, : 3 * WIDTH + LOW])
    for turn in range(LAYERS):
        at = pl.ds(turn * shard, shard)
        standard, scale_inv = norm_parts(rows_of(messages.at[turn], shard))
        part = grad_normed[turn * shard : (turn + 1) * shard]
        gn[at, :] += norm_back(part, standard, scale_inv, gains[0:1, :])
    stores.append(pltpu.make_async_copy(gn, gm_h, out_sem.at[0]))
    stores[-1].start()
    load_rest[-1].wait()
    normed_mine = picked(normed, places)
    down_v = dot_t(dv[...], up_v[...]).astype(BF16)
    terms[0] = dot(down_q.T[:16], normed_mine[:, :WIDTH])[:RANK]
    terms[1] = adapter_scale * dot(normed_mine[:, WIDTH:].T[:16], dq[...])[:RANK]
    terms[2] = dot(down_v.T[:16], normed[:, :WIDTH])[LOW_V : LOW_V + RANK]
    terms[3] = adapter_scale * dot(normed[:, WIDTH:].T[:16], dv[...])[LOW_V : LOW_V + RANK]
    for store in stores:
        store.wait()


def closing_kernel(shard, gains, *refs):
    pieces, refs = refs[:LAYERS], refs[LAYERS:]
    gm, outs, refs = refs[0], refs[1 : 1 + NEAR], refs[1 + NEAR :]
    received, grads = refs[:-LAYERS], refs[-LAYERS:]
    for turn in range(LAYERS):
        at = slice(turn * shard, (turn + 1) * shard)
        total = received[0][at, :].astype(F32)
        for other in received[1:]:
            total = total + other[at, :].astype(F32)
        standard, scale_inv = norm_parts(rows_of(pieces[turn], shard))
        grad_rows = gm[at, :] + norm_back(total, standard, scale_inv, gains[0:1, :])
        grads[turn][:shard, :] = grad_rows.astype(BF16)
        if turn < NEAR:
            grads[turn][shard:, :] = outs[turn][...]


def place_kernel(shard, spot, *refs):
    backs, outs, (input_grad, block_output) = far_first(refs[:LAYERS]), refs[LAYERS:-2], refs[-2:]
    for turn in range(LAYERS):
        slot = spot[0] ^ turn
        input_grad[slot] = backs[turn][:shard, :]
        block_output[slot] = backs[turn][shard:, :] if turn < NEAR else outs[turn - NEAR][...]


def cut_rows(whole, slot, message, first, shard):
    for part in range(WIDTH // 128):
        at = slice(first + part * shard, first + (part + 1) * shard)
        message[at, :] = whole[slot, :, part * 128 : (part + 1) * 128]


def pack_kernel(shard, group, docs, whole, *messages):
    home = lax.axis_index("blk") // group
    for turn in range(LAYERS):
        slot = home ^ turn
        cut_rows(whole, slot, messages[turn], 0, shard)
        row = docs[pl.ds(slot, 1), :]
        high = row >> 5
        both = jnp.concatenate([high, row - (high << 5)], axis=0).astype(F32)
        if shard < 128:
            both = jnp.concatenate([both, jnp.zeros((2, 128 - shard), F32)], axis=1)
        both = jnp.concatenate([both, jnp.zeros((14, 128), F32)], axis=0)
        messages[turn][WIDTH // 128 * shard :, :] = both.astype(BF16)


def cut_kernel(shard, spot, pulls, adapters, *refs):
    pieces, (low, up_q, up_v) = refs[:LAYERS], refs[LAYERS:]
    for turn in range(LAYERS):
        cut_rows(pulls, spot[0] ^ turn, pieces[turn], 0, shard)
    none = jnp.zeros((RANK, WIDTH), F32)
    rounded = [adapters[place].astype(BF16).astype(F32) for place in range(4)]
    tail = jnp.zeros((LOW - 2 * LOW_V, WIDTH), F32)
    low[...] = jnp.concatenate([rounded[0], none, rounded[2], none, tail], axis=0).astype(BF16)
    up_q[...] = jnp.concatenate([adapter_scale * rounded[1], none, none, none, tail], axis=0).astype(BF16)
    up_v[...] = jnp.concatenate([none, none, adapter_scale * rounded[3], none, tail], axis=0).astype(BF16)


def adam_update(adapter_grads, adapters, moment_one, moment_two):
    norm_total = jnp.sqrt(jnp.sum(adapter_grads * adapter_grads))
    clipped_grads = adapter_grads * jnp.minimum(1.0, math.sqrt(4.0 * RANK * WIDTH) / norm_total)
    new_moment_one = beta_first * moment_one + (1.0 - beta_first) * clipped_grads
    new_moment_two = beta_second * moment_two + (1.0 - beta_second) * clipped_grads * clipped_grads
    first_hat = new_moment_one / (1.0 - beta_first**step_count)
    second_hat = new_moment_two / (1.0 - beta_second**step_count)
    new_adapters = adapters - learn_rate * (
        first_hat / (jnp.sqrt(second_hat) + adam_floor) + decay_rate * adapters
    )
    return (clipped_grads, new_adapters, new_moment_one, new_moment_two)


VM = pl.BlockSpec(memory_space=pltpu.VMEM)
SM = pl.BlockSpec(memory_space=pltpu.SMEM)
ANY = pl.BlockSpec(memory_space=pl.ANY)


def shaped(dtype, *shape):
    return jax.ShapeDtypeStruct(shape, dtype)


class Routes:
    def __init__(self, slots, blks):
        self.slots, self.blks = slots, blks
        self.group = blks // LAYERS
        self.chips = self.group // 2

    def gathering(self, turn):
        pairs = []
        for slot in range(self.slots):
            for blk in range(self.blks):
                layer, member = blk // self.group, blk % self.group
                target = (2 * (layer ^ turn) + slot % 2) * self.chips + member // 2
                pairs.append((slot * self.blks + blk, (slot - slot % 2 + member % 2) * self.blks + target))
        return pairs

    def returning(self, turn):
        return [(target, source) for source, target in self.gathering(turn)]

    def within(self, other):
        pairs = []
        for slot in range(self.slots):
            for blk in range(self.blks):
                to_slot, to_blk = slot ^ (other & 1), blk ^ (other >> 1)
                pairs.append((slot * self.blks + blk, to_slot * self.blks + to_blk))
        return pairs

    def reaches(self):
        along = [self.blks >> step for step in range(1, self.blks.bit_length())]
        across = [self.blks << step for step in range(self.slots.bit_length() - 1)]
        return across[::-1] + along[2:], [along[1], along[0], along[0] + along[1]]

    def spot(self, slot, blk):
        own = blk // self.chips // 2
        member = (blk % self.chips) * 2 + slot % 2
        return own, member


def body(
    routes,
    activations,
    cotangent,
    norm_gains,
    norm_shifts,
    w_qkv,
    query_value_bias,
    w_out,
    resid_bias,
    w_fc,
    fc_bias,
    w_proj,
    doc_ids,
    adapters,
    moment_one,
    moment_two,
):
    axes = ("slot", "blk")
    group = routes.group
    shard = activations.shape[1]
    span, rows, length = group * shard, LAYERS * shard, LAYERS * group * shard
    width_fc = w_fc.shape[1]
    slot, blk = lax.axis_index("slot"), lax.axis_index("blk")
    home = blk // group
    own, member = routes.spot(slot, blk)
    spot = jnp.stack([home, own, member]).astype(jnp.int32)
    turns = range(LAYERS)

    def pick(whole, turn):
        return lax.dynamic_index_in_dim(whole, home ^ turn, 0, keepdims=False)

    def send(piece, pairs):
        return lax.ppermute(piece, axes, pairs)

    params = pltpu.CompilerParams(vmem_limit_bytes=VMEM_BYTES)
    piece_shape = shaped(BF16, shard, WIDTH)
    part_rows = WIDTH // 128 * shard
    message_rows = part_rows + 16

    messages = pl.pallas_call(
        partial(pack_kernel, shard, group),
        in_specs=[VM] * 2,
        out_specs=[VM] * LAYERS,
        out_shape=[shaped(BF16, message_rows, 128)] * LAYERS,
        name="pack",
    )(doc_ids, activations)
    x_own = [send(messages[turn], routes.gathering(turn)) for turn in turns]
    *cuts, low, up_q, up_v = pl.pallas_call(
        partial(cut_kernel, shard),
        in_specs=[SM, VM, VM],
        out_specs=[VM] * (LAYERS + 3),
        out_shape=[shaped(BF16, part_rows, 128)] * LAYERS + [shaped(BF16, LOW, WIDTH)] * 3,
        name="cut",
    )(spot, cotangent, adapters)
    x_own = [lax.optimization_barrier((piece, low))[0] for piece in x_own]
    pulls = [None] * LAYERS
    for turn in range(NEAR):
        cuts[turn] = lax.optimization_barrier((cuts[turn], x_own[:NEAR]))[0]
        pulls[turn] = send(cuts[turn], routes.gathering(turn))
    for turn in range(NEAR, LAYERS):
        x_own[turn] = lax.optimization_barrier((x_own[turn], pulls[:NEAR]))[0]
        cuts[turn] = lax.optimization_barrier((cuts[turn], x_own[turn]))[0]
        pulls[turn] = send(cuts[turn], routes.gathering(turn))
    pieces = [None] * (LAYERS * group)
    for turn in turns:
        pieces[turn * group] = x_own[turn]
        for other in range(1, group):
            pieces[turn * group + other] = send(x_own[turn], routes.within(other))

    forward = pl.pallas_call(
        partial(forward_kernel, group, shard),
        in_specs=[SM] + [VM] * 8 + [ANY] * (LAYERS * group + 4),
        out_specs=[ANY] * (LAYERS + 7) + [VM] * 2,
        out_shape=[piece_shape] * LAYERS
        + [
            shaped(BF16, length, WIDTH),
            shaped(BF16, length, WIDTH),
            shaped(BF16, WIDTH, 2 * rows),
            shaped(F32, WIDTH, rows),
            shaped(F32, rows, WIDTH),
            shaped(BF16, rows, width_fc),
            shaped(BF16, length, WIDTH + LOW),
            shaped(F32, PAIRS, LAYERS, 2 * shard),
            shaped(jnp.int32, LAYERS, 1, shard),
        ],
        scratch_shapes=[
            pltpu.VMEM((LAYERS * group, message_rows, 128), BF16),
            pltpu.VMEM((length, WIDTH + LOW), BF16),
            pltpu.VMEM((length, WIDTH), BF16),
            pltpu.VMEM((length, WIDTH), BF16),
            pltpu.VMEM((FORWARD_PAIRS, VROWS, length), BF16),
            pltpu.VMEM((rows, WIDTH), BF16),
            pltpu.VMEM((WIDTH, 2 * rows), BF16),
            pltpu.VMEM((block_start(LAYERS) * span, 2 * shard), F32),
            pltpu.VMEM((WIDTH, rows), F32),
            pltpu.VMEM((rows, WIDTH), BF16),
            pltpu.VMEM((rows, WIDTH), F32),
            pltpu.VMEM((rows, WIDTH), BF16),
            pltpu.VMEM((rows, WIDTH), F32),
            pltpu.VMEM((rows, width_fc), BF16),
            pltpu.VMEM((rows, WIDTH), BF16),
            pltpu.VMEM((WIDTH + LOW, width_fc), BF16),
            pltpu.VMEM((WIDTH, WIDTH), BF16),
            pltpu.VMEM((width_fc, WIDTH), BF16),
            pltpu.SemaphoreType.DMA((LAYERS * group,)),
            pltpu.SemaphoreType.DMA((6,)),
            pltpu.SemaphoreType.DMA((7 + LAYERS,)),
            pltpu.SemaphoreType.DMA((width_fc // 1024,)),
        ],
        compiler_params=params,
        cost_estimate=pl.CostEstimate(flops=22 * 10**9, bytes_accessed=40 * 2**20, transcendentals=0),
        name="forward",
    )
    results = forward(
        spot,
        norm_gains,
        norm_shifts,
        query_value_bias,
        resid_bias,
        fc_bias.reshape(1, width_fc),
        low,
        up_q,
        up_v,
        *far_first(pieces, group),
        w_qkv,
        w_out,
        w_fc,
        w_proj,
    )
    out_pieces = results[:LAYERS]
    keys, values, spread_q, attended_t, middle, slope, normed, log_total, docs = results[LAYERS:]
    outs = [send(out_pieces[turn], routes.returning(turn)) for turn in range(NEAR, LAYERS)]

    parts = width_fc // 1024
    backward = pl.pallas_call(
        partial(backward_kernel, group, shard),
        in_specs=[SM] + [VM] * 6 + [ANY] * (2 * LAYERS + 11),
        out_specs=[ANY] * group + [VM],
        out_shape=[shaped(F32, rows, WIDTH)]
        + [shaped(BF16, rows, WIDTH)] * (group - 1)
        + [shaped(F32, 4, RANK, WIDTH)],
        scratch_shapes=[
            pltpu.VMEM((rows, WIDTH), BF16),
            pltpu.VMEM((rows, width_fc), BF16),
            pltpu.VMEM((rows, width_fc), BF16),
            pltpu.VMEM((rows, WIDTH), F32),
            pltpu.VMEM((rows, WIDTH), F32),
            pltpu.VMEM((rows, WIDTH), BF16),
            pltpu.VMEM((length, WIDTH), BF16),
            pltpu.VMEM((length, WIDTH), BF16),
            pltpu.VMEM((WIDTH, 2 * rows), BF16),
            pltpu.VMEM((WIDTH, rows), F32),
            pltpu.VMEM((block_start(LAYERS) * span, 2 * shard), F32),
            pltpu.VMEM((BACKWARD_PAIRS, PAIR, length), BF16),
            pltpu.VMEM((BACKWARD_PAIRS, PAIR, 2 * rows), BF16),
            pltpu.VMEM((rows, WIDTH), BF16),
            pltpu.VMEM((BACKWARD_PAIRS, PAIR, 2 * shard), F32),
            pltpu.VMEM((length, WIDTH), BF16),
            pltpu.VMEM((length, WIDTH), BF16),
            pltpu.VMEM((width_fc, WIDTH), BF16),
            pltpu.VMEM((WIDTH, width_fc), BF16),
            pltpu.VMEM((WIDTH, WIDTH), BF16),
            pltpu.VMEM((length, WIDTH + LOW), BF16),
            pltpu.VMEM((LAYERS, WIDTH // 128 * shard, 128), BF16),
            pltpu.SemaphoreType.DMA((LAYERS + 2 * parts + 10,)),
            pltpu.SemaphoreType.DMA((group,)),
        ],
        compiler_params=pltpu.CompilerParams(vmem_limit_bytes=BACK_BYTES),
        cost_estimate=pl.CostEstimate(flops=24 * 10**9, bytes_accessed=40 * 2**20, transcendentals=0),
        name="backward",
    )
    results = backward(
        spot,
        docs,
        norm_gains,
        log_total,
        low,
        up_q,
        up_v,
        *pulls,
        *x_own,
        slope,
        middle,
        spread_q,
        attended_t,
        w_proj,
        w_fc,
        w_out,
        w_qkv,
        keys,
        values,
        normed,
    )
    grad_middle, grad_others, terms = results[0], results[1:-1], results[-1]
    outs, grad_others = lax.optimization_barrier((outs, grad_others))
    received = [send(grad_others[other - 1], routes.within(other)) for other in range(1, group)]

    devices = routes.slots * routes.blks

    def partner(part, reach):
        return send(part, [(device, device ^ reach) for device in range(devices)])

    grad_pieces = pl.pallas_call(
        partial(closing_kernel, shard),
        in_specs=[VM] * (LAYERS + 2 + NEAR + group - 1),
        out_specs=[VM] * LAYERS,
        out_shape=[shaped(BF16, 2 * shard if turn < NEAR else shard, WIDTH) for turn in turns],
        compiler_params=pltpu.CompilerParams(vmem_limit_bytes=SMALL_BYTES),
        cost_estimate=pl.CostEstimate(flops=10**7, bytes_accessed=6 * 2**20, transcendentals=0),
        name="closing",
    )(norm_gains, *x_own, grad_middle, *out_pieces[:NEAR], *received)
    backs = [None] * LAYERS
    for turn in turns:
        backs[turn] = send(grad_pieces[turn], routes.returning(turn))
    one_by_one, at_once = routes.reaches()
    terms = lax.optimization_barrier((terms, grad_pieces[0]))[0]
    for place, reach in enumerate(one_by_one):
        if place == len(one_by_one) - 1:
            terms = lax.optimization_barrier((terms, backs[0]))[0]
        terms = terms + partner(terms, reach)
    sums = [terms] + [partner(terms, reach) for reach in at_once]
    while len(sums) > 1:
        sums = [one + two for one, two in zip(sums[::2], sums[1::2])]
    terms = sums[0]
    clipped_grads, new_adapters, new_moment_one, new_moment_two = adam_update(
        terms, adapters, moment_one, moment_two
    )

    input_grad, block_output = pl.pallas_call(
        partial(place_kernel, shard),
        in_specs=[SM] + [VM] * (2 * LAYERS - NEAR),
        out_specs=[VM] * 2,
        out_shape=[shaped(BF16, LAYERS, shard, WIDTH)] * 2,
        compiler_params=pltpu.CompilerParams(vmem_limit_bytes=SMALL_BYTES),
        cost_estimate=pl.CostEstimate(flops=0, bytes_accessed=4 * 2**20, transcendentals=0),
        name="place",
    )(spot, *far_first(backs), *outs)
    return (block_output, input_grad, clipped_grads, new_adapters, new_moment_one, new_moment_two)


def solution(mesh):
    routes = Routes(mesh.shape["slot"], mesh.shape["blk"])
    rows = P("slot", "blk", None)
    placed = (rows, rows) + (P(),) * 9 + (P("slot", "blk"),) + (P(),) * 3
    return jax.shard_map(
        partial(body, routes),
        mesh=mesh,
        in_specs=placed,
        out_specs=(rows, rows, P(), P(), P(), P()),
        check_vma=False,
    )
```

```python
from functools import partial
import math

import jax
import jax.numpy as jnp
from jax import lax
from jax.experimental import pallas as pl
from jax.experimental.pallas import tpu as pltpu
from jax.sharding import PartitionSpec as P

WIDTH = 1024
HEADS = 16
HEAD_DIM = 64
RANK = 4
LAYERS = 4
PAIRS = HEADS // 2
PAIR = 2 * HEAD_DIM
LOW = 128
LOW_V = 8
FORWARD_PAIRS = 4
BACKWARD_PAIRS = 4
NEAR = 2
VROWS = PAIR + 16

norm_floor = 1e-05
adapter_scale = 8.0
learn_rate = 0.005
beta_first = 0.9
beta_second = 0.999
adam_floor = 1e-08
decay_rate = 0.01
step_count = 100
masked_score = -1e30

F32 = jnp.float32
BF16 = jnp.bfloat16
GELU_C = math.sqrt(2.0 / math.pi)
VMEM_BYTES = 57 * 2**20
BACK_BYTES = 60 * 2**20
SMALL_BYTES = 16 * 2**20


def dot(left, right):
    return jnp.dot(left, right, preferred_element_type=F32)


def dot_t(left, right):
    return lax.dot_general(left, right, (((1,), (1,)), ((), ())), preferred_element_type=F32)


def norm_parts(rows):
    center = rows - jnp.mean(rows, axis=-1, keepdims=True)
    scale_inv = lax.rsqrt(jnp.mean(center * center, axis=-1, keepdims=True) + norm_floor)
    return center * scale_inv, scale_inv


def norm_back(grad_out, standard, scale_inv, gain):
    scaled = grad_out * gain
    return scale_inv * (
        scaled
        - jnp.mean(scaled, axis=-1, keepdims=True)
        - standard * jnp.mean(scaled * standard, axis=-1, keepdims=True)
    )


def gelu_parts(hidden):
    square = hidden * hidden
    bend = jnp.tanh(hidden * (GELU_C + (GELU_C * 0.044715) * square))
    half = 0.5 + 0.5 * bend
    slope = half + hidden * (1.0 - bend * bend) * (0.5 * GELU_C + (1.5 * GELU_C * 0.044715) * square)
    return hidden * half, slope


def block_start(layer):
    return layer * (layer + 1) // 2


def fill_bias(spot, docs, bias, shard, span):
    own, member = spot[1], spot[2]
    for layer in range(LAYERS):
        row = docs[own ^ layer]
        starts = jnp.concatenate([row, row], axis=1)
        keys = span * (layer + 1)
        key_at = lax.broadcasted_iota(jnp.int32, (keys, 2 * shard), 0)
        query_at = lax.broadcasted_iota(jnp.int32, (1, 2 * shard), 1)
        query_at = jnp.where(query_at >= shard, query_at - shard, query_at)
        query_at = query_at + (layer * span + member * shard)
        allowed = (key_at >= starts) & (key_at <= query_at)
        bias[pl.ds(block_start(layer) * span, keys), :] = jnp.where(allowed, 0.0, masked_score)


def spread(block, shard):
    none = jnp.zeros((HEAD_DIM, shard), block.dtype)
    return jnp.concatenate(
        [
            jnp.concatenate([block[:HEAD_DIM], none], axis=1),
            jnp.concatenate([none, block[HEAD_DIM:]], axis=1),
        ],
        axis=0,
    )


def gather_diagonal(block, shard):
    return jnp.concatenate([block[:HEAD_DIM, :shard], block[HEAD_DIM:PAIR, shard:]], axis=0)


def pipelined(tasks, first, second, third):
    ready = first(*tasks[0])
    waiting = None
    for place, task in enumerate(tasks):
        following = first(*tasks[place + 1]) if place + 1 < len(tasks) else None
        weighed = second(*task, *ready)
        if waiting is not None:
            third(*waiting)
        waiting = (*task, *weighed)
        ready = following
    third(*waiting)


def far_first(arrays, each=1):
    return [array for turn in range(LAYERS - 1, -1, -1) for array in arrays[turn * each : (turn + 1) * each]]


def rows_of(message, shard):
    parts = [message[part * shard : (part + 1) * shard, :] for part in range(WIDTH // 128)]
    return jnp.concatenate(parts, axis=1).astype(F32)


def forward_kernel(group, shard, spot, gains, shifts, qv_bias, resid, fc_bias, low, up_q, up_v, *refs):
    pieces, refs = far_first(refs[: LAYERS * group], group), refs[LAYERS * group :]
    wqkv_h, wout_h, wfc_h, wproj_h = refs[:4]
    out_h, refs = refs[4 : 4 + LAYERS], refs[4 + LAYERS :]
    keys_h, values_h, spread_h, attended_h, middle_h, slope_h, normed_h, log_total, docs = refs[:9]
    x, normed, keys, values, values_t, query, spread_q, bias, attended_t, attended = refs[9:19]
    middle, normed_two, total, slope, out, wbuf, wout, wproj = refs[19:27]
    in_sem, w_sem, out_sem, slope_sem = refs[27:]
    span = group * shard
    rows = LAYERS * shard
    width_fc = wfc_h.shape[1]
    own, member = spot[1], spot[2]

    loads = [
        pltpu.make_async_copy(pieces[place].at[pl.ds(0, x.shape[1]), :], x.at[place], in_sem.at[place])
        for place in range(LAYERS * group)
    ]
    for load in loads:
        load.start()
    load_qkv = []
    for place, part in enumerate((1, 2, 0)):
        at = pl.ds(part * WIDTH, WIDTH)
        load_qkv.append(pltpu.make_async_copy(wqkv_h.at[:, at], wbuf.at[pl.ds(0, WIDTH), at], w_sem.at[place]))
    load_qkv[0].start()
    load_out = pltpu.make_async_copy(wout_h, wout, w_sem.at[3])
    load_fc = pltpu.make_async_copy(wfc_h, wbuf.at[pl.ds(0, WIDTH), :], w_sem.at[4])
    load_proj = pltpu.make_async_copy(wproj_h, wproj, w_sem.at[5])
    for turn in range(LAYERS):
        for other in range(group):
            place = turn * group + other
            loads[place].wait()
            if place == LAYERS * group - 1:
                load_qkv[1].start()
                load_qkv[2].start()
            if other == 0:
                numbers = x[place, WIDTH // 128 * shard :, :].astype(F32)
                docs[turn] = (numbers[0:1, :shard] * 32.0 + numbers[1:2, :shard]).astype(jnp.int32)
            standard, _ = norm_parts(rows_of(x.at[place], shard))
            at = pl.ds(pl.multiple_of((own ^ turn) * span + (member ^ other) * shard, shard), shard)
            normed[at, :WIDTH] = (standard * gains[0:1, :] + shifts[0:1, :]).astype(BF16)
    normed[:, WIDTH:] = dot_t(normed[:, :WIDTH], low[...]).astype(BF16)
    wbuf[WIDTH:, :WIDTH] = up_q[...]
    wbuf[WIDTH:, 2 * WIDTH : 3 * WIDTH] = up_v[...]
    half = WIDTH // 2
    load_qkv[0].wait()
    for first in range(0, WIDTH, half):
        at = pl.ds(first, half)
        keys[:, at] = dot(normed[:, :WIDTH], wbuf[:WIDTH, WIDTH + first : WIDTH + first + half]).astype(BF16)
    fill_bias(spot, docs, bias, shard, span)
    load_qkv[1].wait()
    for first in range(0, WIDTH, half):
        at = pl.ds(first, half)
        values[:, at] = (
            dot(normed[...], wbuf[:, 2 * WIDTH + first : 2 * WIDTH + first + half])
            + qv_bias[1:2, at]
        ).astype(BF16)
    own_rows = [pl.ds(pl.multiple_of(layer * span + member * shard, shard), shard) for layer in range(LAYERS)]
    mine = jnp.concatenate([normed[at, :] for at in own_rows], axis=0)
    load_qkv[2].wait()
    query[...] = (
        (dot(mine, wbuf[:, :WIDTH]) + qv_bias[0:1, :]).astype(BF16) * 0.125
    ).astype(BF16)
    load_out.start()
    load_fc.start()
    load_proj.start()
    stores = [
        pltpu.make_async_copy(keys, keys_h, out_sem.at[0]),
        pltpu.make_async_copy(values, values_h, out_sem.at[1]),
        pltpu.make_async_copy(normed, normed_h, out_sem.at[6 + LAYERS]),
    ]
    for store in stores:
        store.start()

    def attend(step, _):
        both = []
        for side in range(FORWARD_PAIRS):
            at = pl.ds(pl.multiple_of((FORWARD_PAIRS * step + side) * PAIR, PAIR), PAIR)
            values_t[side, :PAIR, :] = values[:, at].T
            values_t[side, PAIR:, :] = jnp.ones((VROWS - PAIR, values.shape[0]), BF16)
            for layer in range(LAYERS):
                block = query[layer * shard : (layer + 1) * shard, at].T
                spread_q[at, layer * 2 * shard : (layer + 1) * 2 * shard] = spread(block, shard)
            both.append(at)

        def score(side, layer):
            seen = span * (layer + 1)
            scores = dot(keys[0:seen, both[side]], spread_q[both[side], layer * 2 * shard : (layer + 1) * 2 * shard])
            return (scores + bias[block_start(layer) * span : block_start(layer) * span + seen, :],)

        def weigh(side, layer, scores):
            highest = jnp.max(scores, axis=0, keepdims=True)
            return highest, jnp.exp(scores - highest).astype(BF16)

        def gather(side, layer, highest, weights):
            seen = span * (layer + 1)
            summed = dot(values_t[side, :, 0:seen], weights)
            totals = summed[PAIR : PAIR + 1, :]
            block = gather_diagonal(summed[:PAIR] * (1.0 / totals), shard)
            attended_t[both[side], layer * shard : (layer + 1) * shard] = block
            at = pl.ds(pl.multiple_of((own ^ layer) * shard, shard), shard)
            attended[at, both[side]] = block.T.astype(BF16)
            log_total[FORWARD_PAIRS * step + side, layer : layer + 1, :] = highest + jnp.log(totals)

        tasks = [(side, layer) for side in range(FORWARD_PAIRS) for layer in range(LAYERS)]
        pipelined(tasks, score, weigh, gather)
        return 0

    lax.fori_loop(0, PAIRS // FORWARD_PAIRS, attend, 0)
    stores.append(pltpu.make_async_copy(spread_q, spread_h, out_sem.at[2]))
    stores.append(pltpu.make_async_copy(attended_t, attended_h, out_sem.at[3]))
    for store in stores[3:]:
        store.start()
    load_out.wait()
    branch = dot(attended[...], wout[...]) + resid[0:1, :]
    for turn in range(LAYERS):
        at = pl.ds(turn * shard, shard)
        center = rows_of(x.at[turn * group], shard) + branch[turn * shard : (turn + 1) * shard]
        middle[at, :] = center
        standard, _ = norm_parts(center)
        normed_two[at, :] = (standard * gains[1:2, :] + shifts[1:2, :]).astype(BF16)
    stores.append(pltpu.make_async_copy(middle, middle_h, out_sem.at[4]))
    stores[-1].start()
    load_fc.wait()
    load_proj.wait()
    chunk = 1024
    hidden, acts = {}, {}
    count = width_fc // chunk
    for step in range(count + 2):
        if step < count:
            hidden[step] = dot(normed_two[...], wbuf[:WIDTH, step * chunk : (step + 1) * chunk])
        if 0 <= step - 1 < count:
            at = pl.ds((step - 1) * chunk, chunk)
            act, tilt = gelu_parts(hidden.pop(step - 1) + fc_bias[:, at])
            acts[step - 1] = act.astype(BF16)
            slope[:, at] = tilt.astype(BF16)
            stores.append(pltpu.make_async_copy(slope.at[:, at], slope_h.at[:, at], slope_sem.at[step - 1]))
            stores[-1].start()
        if 0 <= step - 2:
            part = dot(acts.pop(step - 2), wproj[(step - 2) * chunk : (step - 1) * chunk, :])
            if step - 2 == 0:
                total[...] = part
            elif step - 1 < count:
                total[...] += part
            else:
                out[...] = (middle[...] + total[...] + part + resid[1:2, :]).astype(BF16)
    for turn in range(LAYERS):
        stores.append(
            pltpu.make_async_copy(out.at[pl.ds(turn * shard, shard), :], out_h[turn], out_sem.at[6 + turn])
        )
        stores[-1].start()
    for store in stores:
        store.wait()


def backward_kernel(group, shard, spot, docs, gains, log_total, low, up_q, up_v, *refs):
    pulls, refs = refs[:LAYERS], refs[LAYERS:]
    pieces, refs = refs[:LAYERS], refs[LAYERS:]
    slope_h, middle_h, spread_h, attended_h, wproj_h, wfc_h, wout_h, wqkv_h = refs[:8]
    keys_h, values_h, normed_h, refs = refs[8], refs[9], refs[10], refs[11:]
    gm_h, refs = refs[0], refs[1:]
    other_h, terms, refs = refs[: group - 1], refs[group - 1], refs[group:]
    pull, slope, grad_hidden, gn, middle, grad_att, keys, values, spread_q, attended_t = refs[:10]
    bias, keys_t, spread_g, dq, dq_t, dk, dv, wproj, wfc, wout, normed, messages = refs[10:22]
    in_sem, out_sem = refs[22:]
    span = group * shard
    rows = LAYERS * shard
    length = LAYERS * span
    width_fc = wfc_h.shape[1]
    chunk = 1024
    own, member = spot[1], spot[2]

    part_rows = WIDTH // 128 * shard
    load_pull = [
        pltpu.make_async_copy(
            pulls[turn], messages.at[turn], in_sem.at[turn]
        )
        for turn in range(LAYERS)
    ]
    load_proj, load_slope = [], []
    for part in range(width_fc // chunk):
        at = pl.ds(part * chunk, chunk)
        load_proj.append(pltpu.make_async_copy(wproj_h.at[at, :], wproj.at[at, :], in_sem.at[LAYERS + 2 * part]))
        load_slope.append(
            pltpu.make_async_copy(slope_h.at[:, at], slope.at[:, at], in_sem.at[LAYERS + 2 * part + 1])
        )
    base = LAYERS + 2 * (width_fc // chunk)
    load_rest = [
        pltpu.make_async_copy(source, target, in_sem.at[base + place])
        for place, (source, target) in enumerate(
            (
                (wfc_h.at[pl.ds(0, WIDTH // 2), :], wfc.at[pl.ds(0, WIDTH // 2), :]),
                (wfc_h.at[pl.ds(WIDTH // 2, WIDTH // 2), :], wfc.at[pl.ds(WIDTH // 2, WIDTH // 2), :]),
                (middle_h, middle),
                (wout_h, wout),
                (keys_h, keys),
                (values_h, values),
                (spread_h, spread_q),
                (attended_h, attended_t),
                (normed_h, normed),
            )
        )
    ]
    for load in load_pull:
        load.start()
    for part in range(2):
        load_proj[part].start()
        load_slope[part].start()
    for turn in range(LAYERS):
        load_pull[turn].wait()
        pull[turn * shard : (turn + 1) * shard, :] = rows_of(messages.at[turn], shard).astype(BF16)
    for part in range(width_fc // chunk):
        at = pl.ds(part * chunk, chunk)
        load_proj[part].wait()
        load_slope[part].wait()
        if part + 2 < width_fc // chunk:
            load_proj[part + 2].start()
            load_slope[part + 2].start()
        else:
            load_rest[part + 2 - width_fc // chunk].start()
        grad_hidden[:, at] = (dot_t(pull[...], wproj[at, :]) * slope[:, at].astype(F32)).astype(BF16)
    for load in load_rest[2:]:
        load.start()
    fill_bias(spot, docs, bias, shard, span)
    half = WIDTH // 2
    for first in range(0, WIDTH, half):
        at = pl.ds(first, half)
        load_rest[first // half].wait()
        gn[:, at] = dot_t(grad_hidden[...], wfc[at, :])
    load_rest[2].wait()
    load_rest[3].wait()
    standard, scale_inv = norm_parts(middle[...])
    grad_middle = pull[...].astype(F32) + norm_back(gn[...], standard, scale_inv, gains[1:2, :])
    gn[...] = grad_middle
    grad_att[...] = dot_t(grad_middle.astype(BF16), wout[...]).astype(BF16)
    load_last = [pltpu.make_async_copy(wqkv_h, wfc.at[:, pl.ds(0, 3 * WIDTH)], in_sem.at[base + len(load_rest)])]
    load_last.extend(
        pltpu.make_async_copy(pieces[turn].at[pl.ds(0, part_rows), :], messages.at[turn], in_sem.at[turn])
        for turn in range(LAYERS)
    )
    for load in load_last:
        load.start()
    for load in load_rest[4:-1]:
        load.wait()

    def attend(step, _):
        both = [pl.ds(pl.multiple_of((BACKWARD_PAIRS * step + side) * PAIR, PAIR), PAIR) for side in range(BACKWARD_PAIRS)]
        for side in range(BACKWARD_PAIRS):
            keys_t[side] = keys[:, both[side]].T
        deltas = {}
        totals = {}

        def score(side, layer, first):
            cut = pl.ds(layer * 2 * shard, 2 * shard)
            if first == 0:
                at = pl.ds(pl.multiple_of((own ^ layer) * shard, shard), shard)
                block = grad_att[at, both[side]].T
                product = block.astype(F32) * attended_t[both[side], layer * shard : (layer + 1) * shard]
                deltas[side, layer] = jnp.concatenate(
                    [
                        jnp.sum(product[:HEAD_DIM], axis=0, keepdims=True),
                        jnp.sum(product[HEAD_DIM:], axis=0, keepdims=True),
                    ],
                    axis=1,
                )
                spread_g[side, :, layer * 2 * shard : (layer + 1) * 2 * shard] = spread(block, shard)
            key_rows = keys[first : first + span, both[side]]
            value_rows = values[first : first + span, both[side]]
            start = block_start(layer) * span + first
            scores = dot(key_rows, spread_q[both[side], cut]) + bias[start : start + span, :]
            return scores, dot(value_rows, spread_g[side, :, cut])

        def weigh(side, layer, first, scores, grad_chances):
            chances = jnp.exp(scores - log_total[BACKWARD_PAIRS * step + side, layer : layer + 1, :])
            grad_scores = chances * (grad_chances - deltas[side, layer])
            return chances.astype(BF16), grad_scores.astype(BF16)

        def gather(side, layer, first, chances, grad_scores):
            cut = pl.ds(layer * 2 * shard, 2 * shard)
            back_v = dot_t(spread_g[side, :, cut], chances)
            back_k = dot_t(spread_q[both[side], cut], grad_scores)
            back_q = dot(keys_t[side, :, first : first + span], grad_scores)
            part = first // span
            if layer == part:
                totals[side, part] = (back_k, back_v)
            else:
                before = totals[side, part]
                totals[side, part] = (before[0] + back_k, before[1] + back_v)
            if first > 0:
                back_q = back_q + dq_t[side]
            if layer == part:
                at = pl.ds(pl.multiple_of((own ^ layer) * shard, shard), shard)
                dq[at, both[side]] = (gather_diagonal(back_q, shard) * 0.125).T.astype(BF16)
            else:
                dq_t[side] = back_q
            if layer == LAYERS - 1:
                done_k, done_v = totals.pop((side, part))
                dk[first : first + span, both[side]] = done_k.T.astype(BF16)
                dv[first : first + span, both[side]] = done_v.T.astype(BF16)

        tasks = [
            (side, layer, part * span) for side in range(BACKWARD_PAIRS) for layer in range(LAYERS) for part in range(layer + 1)
        ]
        pipelined(tasks, score, weigh, gather)
        return 0

    lax.fori_loop(0, PAIRS // BACKWARD_PAIRS, attend, 0)
    for load in load_last:
        load.wait()

    def member_rows(other):
        return [
            pl.ds(pl.multiple_of((own ^ turn) * span + (member ^ other) * shard, shard), shard)
            for turn in range(LAYERS)
        ]

    def picked(source, places):
        return jnp.concatenate([source[at, :] for at in places], axis=0)

    stores = []
    wfc[:, 3 * WIDTH : 3 * WIDTH + LOW] = low[...].T
    for other in range(1, group):
        places = member_rows(other)
        part_v = picked(dv, places)
        down = dot_t(part_v, up_v[...]).astype(BF16)
        stack = jnp.concatenate([picked(dk, places), part_v, down], axis=1)
        at = pl.ds((other - 1) * WIDTH, WIDTH)
        slope[:, at] = dot_t(stack, wfc[:, WIDTH : 3 * WIDTH + LOW]).astype(BF16)
        stores.append(pltpu.make_async_copy(slope.at[:, at], other_h[other - 1], out_sem.at[other]))
        stores[-1].start()
    places = member_rows(0)
    part_v = picked(dv, places)
    down_q = dot_t(dq[...], up_q[...]).astype(BF16)
    down = down_q + dot_t(part_v, up_v[...]).astype(BF16)
    stack = jnp.concatenate([dq[...], picked(dk, places), part_v, down], axis=1)
    grad_normed = dot_t(stack, wfc[:, : 3 * WIDTH + LOW])
    for turn in range(LAYERS):
        at = pl.ds(turn * shard, shard)
        standard, scale_inv = norm_parts(rows_of(messages.at[turn], shard))
        part = grad_normed[turn * shard : (turn + 1) * shard]
        gn[at, :] += norm_back(part, standard, scale_inv, gains[0:1, :])
    stores.append(pltpu.make_async_copy(gn, gm_h, out_sem.at[0]))
    stores[-1].start()
    load_rest[-1].wait()
    normed_mine = picked(normed, places)
    down_v = dot_t(dv[...], up_v[...]).astype(BF16)
    terms[0] = dot(down_q.T[:16], normed_mine[:, :WIDTH])[:RANK]
    terms[1] = adapter_scale * dot(normed_mine[:, WIDTH:].T[:16], dq[...])[:RANK]
    terms[2] = dot(down_v.T[:16], normed[:, :WIDTH])[LOW_V : LOW_V + RANK]
    terms[3] = adapter_scale * dot(normed[:, WIDTH:].T[:16], dv[...])[LOW_V : LOW_V + RANK]
    for store in stores:
        store.wait()


def closing_kernel(shard, gains, *refs):
    pieces, refs = refs[:LAYERS], refs[LAYERS:]
    gm, outs, refs = refs[0], refs[1 : 1 + NEAR], refs[1 + NEAR :]
    received, grads = refs[:-LAYERS], refs[-LAYERS:]
    for turn in range(LAYERS):
        at = slice(turn * shard, (turn + 1) * shard)
        total = received[0][at, :].astype(F32)
        for other in received[1:]:
            total = total + other[at, :].astype(F32)
        standard, scale_inv = norm_parts(rows_of(pieces[turn], shard))
        grad_rows = gm[at, :] + norm_back(total, standard, scale_inv, gains[0:1, :])
        grads[turn][:shard, :] = grad_rows.astype(BF16)
        if turn < NEAR:
            grads[turn][shard:, :] = outs[turn][...]


def place_kernel(shard, spot, *refs):
    backs, outs, (input_grad, block_output) = far_first(refs[:LAYERS]), refs[LAYERS:-2], refs[-2:]
    for turn in range(LAYERS):
        slot = spot[0] ^ turn
        input_grad[slot] = backs[turn][:shard, :]
        block_output[slot] = backs[turn][shard:, :] if turn < NEAR else outs[turn - NEAR][...]


def cut_rows(whole, slot, message, first, shard):
    for part in range(WIDTH // 128):
        at = slice(first + part * shard, first + (part + 1) * shard)
        message[at, :] = whole[slot, :, part * 128 : (part + 1) * 128]


def pack_kernel(shard, group, docs, whole, *messages):
    home = lax.axis_index("blk") // group
    for turn in range(LAYERS):
        slot = home ^ turn
        cut_rows(whole, slot, messages[turn], 0, shard)
        row = docs[pl.ds(slot, 1), :]
        high = row >> 5
        both = jnp.concatenate([high, row - (high << 5)], axis=0).astype(F32)
        if shard < 128:
            both = jnp.concatenate([both, jnp.zeros((2, 128 - shard), F32)], axis=1)
        both = jnp.concatenate([both, jnp.zeros((14, 128), F32)], axis=0)
        messages[turn][WIDTH // 128 * shard :, :] = both.astype(BF16)


def cut_kernel(shard, spot, pulls, adapters, *refs):
    pieces, (low, up_q, up_v) = refs[:LAYERS], refs[LAYERS:]
    for turn in range(LAYERS):
        cut_rows(pulls, spot[0] ^ turn, pieces[turn], 0, shard)
    none = jnp.zeros((RANK, WIDTH), F32)
    rounded = [adapters[place].astype(BF16).astype(F32) for place in range(4)]
    tail = jnp.zeros((LOW - 2 * LOW_V, WIDTH), F32)
    low[...] = jnp.concatenate([rounded[0], none, rounded[2], none, tail], axis=0).astype(BF16)
    up_q[...] = jnp.concatenate([adapter_scale * rounded[1], none, none, none, tail], axis=0).astype(BF16)
    up_v[...] = jnp.concatenate([none, none, adapter_scale * rounded[3], none, tail], axis=0).astype(BF16)


def adam_update(adapter_grads, adapters, moment_one, moment_two):
    norm_total = jnp.sqrt(jnp.sum(adapter_grads * adapter_grads))
    clipped_grads = adapter_grads * jnp.minimum(1.0, math.sqrt(4.0 * RANK * WIDTH) / norm_total)
    new_moment_one = beta_first * moment_one + (1.0 - beta_first) * clipped_grads
    new_moment_two = beta_second * moment_two + (1.0 - beta_second) * clipped_grads * clipped_grads
    first_hat = new_moment_one / (1.0 - beta_first**step_count)
    second_hat = new_moment_two / (1.0 - beta_second**step_count)
    new_adapters = adapters - learn_rate * (
        first_hat / (jnp.sqrt(second_hat) + adam_floor) + decay_rate * adapters
    )
    return (clipped_grads, new_adapters, new_moment_one, new_moment_two)


VM = pl.BlockSpec(memory_space=pltpu.VMEM)
SM = pl.BlockSpec(memory_space=pltpu.SMEM)
ANY = pl.BlockSpec(memory_space=pl.ANY)


def shaped(dtype, *shape):
    return jax.ShapeDtypeStruct(shape, dtype)


class Routes:
    def __init__(self, slots, blks):
        self.slots, self.blks = slots, blks
        self.group = blks // LAYERS
        self.chips = self.group // 2

    def gathering(self, turn):
        pairs = []
        for slot in range(self.slots):
            for blk in range(self.blks):
                layer, member = blk // self.group, blk % self.group
                target = (2 * (layer ^ turn) + slot % 2) * self.chips + member // 2
                pairs.append((slot * self.blks + blk, (slot - slot % 2 + member % 2) * self.blks + target))
        return pairs

    def returning(self, turn):
        return [(target, source) for source, target in self.gathering(turn)]

    def within(self, other):
        pairs = []
        for slot in range(self.slots):
            for blk in range(self.blks):
                to_slot, to_blk = slot ^ (other & 1), blk ^ (other >> 1)
                pairs.append((slot * self.blks + blk, to_slot * self.blks + to_blk))
        return pairs

    def reaches(self):
        along = [self.blks >> step for step in range(1, self.blks.bit_length())]
        across = [self.blks << step for step in range(self.slots.bit_length() - 1)]
        return across[::-1] + along[2:], [along[1], along[0], along[0] + along[1]]

    def spot(self, slot, blk):
        own = blk // self.chips // 2
        member = (blk % self.chips) * 2 + slot % 2
        return own, member


def body(
    routes,
    activations,
    cotangent,
    norm_gains,
    norm_shifts,
    w_qkv,
    query_value_bias,
    w_out,
    resid_bias,
    w_fc,
    fc_bias,
    w_proj,
    doc_ids,
    adapters,
    moment_one,
    moment_two,
):
    axes = ("slot", "blk")
    group = routes.group
    shard = activations.shape[1]
    span, rows, length = group * shard, LAYERS * shard, LAYERS * group * shard
    width_fc = w_fc.shape[1]
    slot, blk = lax.axis_index("slot"), lax.axis_index("blk")
    home = blk // group
    own, member = routes.spot(slot, blk)
    spot = jnp.stack([home, own, member]).astype(jnp.int32)
    turns = range(LAYERS)

    def pick(whole, turn):
        return lax.dynamic_index_in_dim(whole, home ^ turn, 0, keepdims=False)

    def send(piece, pairs):
        return lax.ppermute(piece, axes, pairs)

    params = pltpu.CompilerParams(vmem_limit_bytes=VMEM_BYTES)
    piece_shape = shaped(BF16, shard, WIDTH)
    part_rows = WIDTH // 128 * shard
    message_rows = part_rows + 16

    messages = pl.pallas_call(
        partial(pack_kernel, shard, group),
        in_specs=[VM] * 2,
        out_specs=[VM] * LAYERS,
        out_shape=[shaped(BF16, message_rows, 128)] * LAYERS,
        name="pack",
    )(doc_ids, activations)
    x_own = [send(messages[turn], routes.gathering(turn)) for turn in turns]
    *cuts, low, up_q, up_v = pl.pallas_call(
        partial(cut_kernel, shard),
        in_specs=[SM, VM, VM],
        out_specs=[VM] * (LAYERS + 3),
        out_shape=[shaped(BF16, part_rows, 128)] * LAYERS + [shaped(BF16, LOW, WIDTH)] * 3,
        name="cut",
    )(spot, cotangent, adapters)
    x_own = [lax.optimization_barrier((piece, low))[0] for piece in x_own]
    pulls = [None] * LAYERS
    for turn in range(NEAR):
        cuts[turn] = lax.optimization_barrier((cuts[turn], x_own[:NEAR]))[0]
        pulls[turn] = send(cuts[turn], routes.gathering(turn))
    for turn in range(NEAR, LAYERS):
        x_own[turn] = lax.optimization_barrier((x_own[turn], pulls[:NEAR]))[0]
        cuts[turn] = lax.optimization_barrier((cuts[turn], x_own[turn]))[0]
        pulls[turn] = send(cuts[turn], routes.gathering(turn))
    pieces = [None] * (LAYERS * group)
    for turn in turns:
        pieces[turn * group] = x_own[turn]
        for other in range(1, group):
            pieces[turn * group + other] = send(x_own[turn], routes.within(other))

    forward = pl.pallas_call(
        partial(forward_kernel, group, shard),
        in_specs=[SM] + [VM] * 8 + [ANY] * (LAYERS * group + 4),
        out_specs=[ANY] * (LAYERS + 7) + [VM] * 2,
        out_shape=[piece_shape] * LAYERS
        + [
            shaped(BF16, length, WIDTH),
            shaped(BF16, length, WIDTH),
            shaped(BF16, WIDTH, 2 * rows),
            shaped(F32, WIDTH, rows),
            shaped(F32, rows, WIDTH),
            shaped(BF16, rows, width_fc),
            shaped(BF16, length, WIDTH + LOW),
            shaped(F32, PAIRS, LAYERS, 2 * shard),
            shaped(jnp.int32, LAYERS, 1, shard),
        ],
        scratch_shapes=[
            pltpu.VMEM((LAYERS * group, message_rows, 128), BF16),
            pltpu.VMEM((length, WIDTH + LOW), BF16),
            pltpu.VMEM((length, WIDTH), BF16),
            pltpu.VMEM((length, WIDTH), BF16),
            pltpu.VMEM((FORWARD_PAIRS, VROWS, length), BF16),
            pltpu.VMEM((rows, WIDTH), BF16),
            pltpu.VMEM((WIDTH, 2 * rows), BF16),
            pltpu.VMEM((block_start(LAYERS) * span, 2 * shard), F32),
            pltpu.VMEM((WIDTH, rows), F32),
            pltpu.VMEM((rows, WIDTH), BF16),
            pltpu.VMEM((rows, WIDTH), F32),
            pltpu.VMEM((rows, WIDTH), BF16),
            pltpu.VMEM((rows, WIDTH), F32),
            pltpu.VMEM((rows, width_fc), BF16),
            pltpu.VMEM((rows, WIDTH), BF16),
            pltpu.VMEM((WIDTH + LOW, width_fc), BF16),
            pltpu.VMEM((WIDTH, WIDTH), BF16),
            pltpu.VMEM((width_fc, WIDTH), BF16),
            pltpu.SemaphoreType.DMA((LAYERS * group,)),
            pltpu.SemaphoreType.DMA((6,)),
            pltpu.SemaphoreType.DMA((7 + LAYERS,)),
            pltpu.SemaphoreType.DMA((width_fc // 1024,)),
        ],
        compiler_params=params,
        cost_estimate=pl.CostEstimate(flops=22 * 10**9, bytes_accessed=40 * 2**20, transcendentals=0),
        name="forward",
    )
    results = forward(
        spot,
        norm_gains,
        norm_shifts,
        query_value_bias,
        resid_bias,
        fc_bias.reshape(1, width_fc),
        low,
        up_q,
        up_v,
        *far_first(pieces, group),
        w_qkv,
        w_out,
        w_fc,
        w_proj,
    )
    out_pieces = results[:LAYERS]
    keys, values, spread_q, attended_t, middle, slope, normed, log_total, docs = results[LAYERS:]
    outs = [send(out_pieces[turn], routes.returning(turn)) for turn in range(NEAR, LAYERS)]

    parts = width_fc // 1024
    backward = pl.pallas_call(
        partial(backward_kernel, group, shard),
        in_specs=[SM] + [VM] * 6 + [ANY] * (2 * LAYERS + 11),
        out_specs=[ANY] * group + [VM],
        out_shape=[shaped(F32, rows, WIDTH)]
        + [shaped(BF16, rows, WIDTH)] * (group - 1)
        + [shaped(F32, 4, RANK, WIDTH)],
        scratch_shapes=[
            pltpu.VMEM((rows, WIDTH), BF16),
            pltpu.VMEM((rows, width_fc), BF16),
            pltpu.VMEM((rows, width_fc), BF16),
            pltpu.VMEM((rows, WIDTH), F32),
            pltpu.VMEM((rows, WIDTH), F32),
            pltpu.VMEM((rows, WIDTH), BF16),
            pltpu.VMEM((length, WIDTH), BF16),
            pltpu.VMEM((length, WIDTH), BF16),
            pltpu.VMEM((WIDTH, 2 * rows), BF16),
            pltpu.VMEM((WIDTH, rows), F32),
            pltpu.VMEM((block_start(LAYERS) * span, 2 * shard), F32),
            pltpu.VMEM((BACKWARD_PAIRS, PAIR, length), BF16),
            pltpu.VMEM((BACKWARD_PAIRS, PAIR, 2 * rows), BF16),
            pltpu.VMEM((rows, WIDTH), BF16),
            pltpu.VMEM((BACKWARD_PAIRS, PAIR, 2 * shard), F32),
            pltpu.VMEM((length, WIDTH), BF16),
            pltpu.VMEM((length, WIDTH), BF16),
            pltpu.VMEM((width_fc, WIDTH), BF16),
            pltpu.VMEM((WIDTH, width_fc), BF16),
            pltpu.VMEM((WIDTH, WIDTH), BF16),
            pltpu.VMEM((length, WIDTH + LOW), BF16),
            pltpu.VMEM((LAYERS, WIDTH // 128 * shard, 128), BF16),
            pltpu.SemaphoreType.DMA((LAYERS + 2 * parts + 10,)),
            pltpu.SemaphoreType.DMA((group,)),
        ],
        compiler_params=pltpu.CompilerParams(vmem_limit_bytes=BACK_BYTES),
        cost_estimate=pl.CostEstimate(flops=24 * 10**9, bytes_accessed=40 * 2**20, transcendentals=0),
        name="backward",
    )
    results = backward(
        spot,
        docs,
        norm_gains,
        log_total,
        low,
        up_q,
        up_v,
        *pulls,
        *x_own,
        slope,
        middle,
        spread_q,
        attended_t,
        w_proj,
        w_fc,
        w_out,
        w_qkv,
        keys,
        values,
        normed,
    )
    grad_middle, grad_others, terms = results[0], results[1:-1], results[-1]
    outs, grad_others = lax.optimization_barrier((outs, grad_others))
    received = [send(grad_others[other - 1], routes.within(other)) for other in range(1, group)]

    devices = routes.slots * routes.blks

    def partner(part, reach):
        return send(part, [(device, device ^ reach) for device in range(devices)])

    grad_pieces = pl.pallas_call(
        partial(closing_kernel, shard),
        in_specs=[VM] * (LAYERS + 2 + NEAR + group - 1),
        out_specs=[VM] * LAYERS,
        out_shape=[shaped(BF16, 2 * shard if turn < NEAR else shard, WIDTH) for turn in turns],
        compiler_params=pltpu.CompilerParams(vmem_limit_bytes=SMALL_BYTES),
        cost_estimate=pl.CostEstimate(flops=10**7, bytes_accessed=6 * 2**20, transcendentals=0),
        name="closing",
    )(norm_gains, *x_own, grad_middle, *out_pieces[:NEAR], *received)
    backs = [None] * LAYERS
    for turn in turns:
        backs[turn] = send(grad_pieces[turn], routes.returning(turn))
    one_by_one, at_once = routes.reaches()
    terms = lax.optimization_barrier((terms, grad_pieces[0]))[0]
    for place, reach in enumerate(one_by_one):
        if place == len(one_by_one) - 1:
            terms = lax.optimization_barrier((terms, backs[0]))[0]
        terms = terms + partner(terms, reach)
    sums = [terms] + [partner(terms, reach) for reach in at_once]
    while len(sums) > 1:
        sums = [one + two for one, two in zip(sums[::2], sums[1::2])]
    terms = sums[0]
    clipped_grads, new_adapters, new_moment_one, new_moment_two = adam_update(
        terms, adapters, moment_one, moment_two
    )

    input_grad, block_output = pl.pallas_call(
        partial(place_kernel, shard),
        in_specs=[SM] + [VM] * (2 * LAYERS - NEAR),
        out_specs=[VM] * 2,
        out_shape=[shaped(BF16, LAYERS, shard, WIDTH)] * 2,
        compiler_params=pltpu.CompilerParams(vmem_limit_bytes=SMALL_BYTES),
        cost_estimate=pl.CostEstimate(flops=0, bytes_accessed=4 * 2**20, transcendentals=0),
        name="place",
    )(spot, *far_first(backs), *outs)
    return (block_output, input_grad, clipped_grads, new_adapters, new_moment_one, new_moment_two)


def solution(mesh):
    routes = Routes(mesh.shape["slot"], mesh.shape["blk"])
    rows = P("slot", "blk", None)
    placed = (rows, rows) + (P(),) * 9 + (P("slot", "blk"),) + (P(),) * 3
    return jax.shard_map(
        partial(body, routes),
        mesh=mesh,
        in_specs=placed,
        out_specs=(rows, rows, P(), P(), P(), P()),
        check_vma=False,
    )
```
